128 devices in a mesh: grp: 4 (over x_hi, core), dev: 32 (over x_lo, y, z).
Axes of the slice: x: 4 (x_hi: 2, x_lo: 2; x = x_hi * 2 + x_lo), y: 4, z: 4, core: 2. Of those that a mesh axis runs over, the one named last changes fastest.
Arguments:
- projections: float32 [24576, 1024], P(('grp', 'dev')), as said below
- row_weights: bfloat16 [24576], P(('grp', 'dev')), may hold values from 0.5 to 2
- partner: int32 [24576], P(('grp', 'dev')), may hold values from 0 to 24575, as said below
Outputs:
- losses: float32 [24576], P(('grp', 'dev'))
- gradient: float32 [24576, 1024], P(('grp', 'dev'))
The draws below stay inside these ranges and needn't reach their ends.
Inputs may be any that keep to these rules, and one draw needn't show every extreme that they name: partner[partner[i]] = i and partner[i] != i for every view i: the views come in pairs, two to an image. `projections`: every row is nonzero.
All inputs are finite; a program needn't handle non-finite values.
Results may differ from the reference program's by a relative error of at most 0.0052.
Values may be sent and summed in bfloat16 or wider, within the bound.
A program may use at most 128 MiB of HBM per device.

```python
import math
import jax
import jax.numpy as jnp
from jax import lax

D = 1024
VIEWS = 24576


cluster_count = 64


def pairing(key):
    shuffled = jax.random.permutation(key, VIEWS).astype(jnp.int32)
    swapped = shuffled.reshape(-1, 2)[:, ::-1].reshape(-1)
    return jnp.zeros((VIEWS,), jnp.int32).at[shuffled].set(swapped)


def draw_partner(key, part):
    return pairing(key)


def draw_projections(key, part):
    partners = pairing(key)
    key = jax.random.fold_in(key, 11)
    key_center, key_member, key_image, key_noise, key_column, key_row = jax.random.split(key, 6)
    image_of = jnp.minimum(jnp.arange(VIEWS, dtype=jnp.int32), partners)
    centers = jax.random.normal(key_center, (cluster_count, D), jnp.float32) * D ** (-0.5)
    member = jax.random.randint(key_member, (VIEWS,), 0, cluster_count)[image_of]
    images = jax.random.normal(key_image, (VIEWS, D), jnp.float32) * D ** (-0.5)
    position = jnp.arange(VIEWS, dtype=jnp.float32) / VIEWS
    noise = jax.random.normal(key_noise, (VIEWS, D), jnp.float32) * D ** (-0.5)
    strength = 0.45 + 0.35 * position
    row_scale = jnp.exp(jax.random.uniform(key_row, (VIEWS, 1), jnp.float32, -0.6931472, 0.6931472))
    column_scale = jnp.exp(jax.random.uniform(key_column, (1, D), jnp.float32, 0.0, 2.3025851))
    blended = strength[:, None] * centers[member] + 0.6 * images[image_of] + 0.55 * noise
    return (blended * column_scale * row_scale * 0.3).astype(jnp.float32)


def steps_of(key, extent, pieces, least, largest):
    factor_of = 1.0
    for dim, blocks in pieces:
        heights = jax.random.uniform(jax.random.fold_in(jax.random.fold_in(key, 6), dim), (blocks,), jnp.float32, least / len(pieces), largest / len(pieces))
        factor_of = factor_of * jnp.repeat(jnp.exp(heights), extent[dim] // blocks).reshape((-1,) + (1,) * (len(extent) - 1 - dim))
    return factor_of


def setup_inputs(seed: int = 0) -> dict:
    arg_keys = jax.random.split(jax.random.key(seed), 4)
    return {
        "projections": draw_projections(jax.random.fold_in(arg_keys[3], 71), 0),
        "row_weights": jnp.clip(jnp.exp(math.log(2.0) - 1.3862944 * jax.random.uniform(arg_keys[1], (VIEWS,), jnp.float32) ** steps_of(arg_keys[1], (VIEWS,), ((0, 128),), -0.2, 0.2)), 0.5, 2.0).astype(jnp.bfloat16),
        "partner": draw_partner(jax.random.fold_in(arg_keys[3], 71), 0),
    }


inv_temp = 10.0
epsilon = 1e-06

def reference(projections, row_weights, partner):
    total_rows = projections.shape[0]
    inv_norm = lax.rsqrt(lax.optimization_barrier(jnp.sum(projections * projections, axis=1, keepdims=True)) + epsilon)
    unit = projections * inv_norm
    views = unit.astype(jnp.bfloat16)
    weights = row_weights.astype(jnp.float32)
    block_rows = math.gcd(total_rows, 512)
    block_count = total_rows // block_rows
    column_ids = jnp.arange(total_rows, dtype=jnp.int32)

    def score_block(block_at):
        row_start = (block_at * block_rows).astype(jnp.int32)
        row_views = lax.dynamic_slice_in_dim(views, row_start, block_rows, 0)
        scores = jnp.dot(row_views, views.T, preferred_element_type=jnp.float32) * inv_temp
        row_ids = row_start + jnp.arange(block_rows, dtype=jnp.int32)
        on_diag = row_ids[:, None] == column_ids[None, :]
        partner_rows = lax.dynamic_slice_in_dim(partner, row_start, block_rows, 0)
        is_partner = partner_rows[:, None] == column_ids[None, :]
        return (row_start, scores, on_diag, is_partner)

    def forward(block_at):
        row_start, scores, on_diag, is_partner = score_block(block_at)
        terms = jnp.where(on_diag, 0.0, jnp.exp(scores - inv_temp))
        return (lax.optimization_barrier(jnp.sum(terms, axis=1)), lax.optimization_barrier(jnp.sum(jnp.where(is_partner, scores, 0.0), axis=1)))
    exp_sums, positive = lax.map(forward, jnp.arange(block_count, dtype=jnp.int32))
    lse = inv_temp + jnp.log(exp_sums.reshape(total_rows))
    losses = lse - positive.reshape(total_rows)

    def backward(block_at):
        row_start, scores, on_diag, is_partner = score_block(block_at)
        row_lse = lax.dynamic_slice_in_dim(lse, row_start, block_rows, 0)
        row_w = lax.dynamic_slice_in_dim(weights, row_start, block_rows, 0)
        toward = jnp.exp(scores - row_lse[:, None])
        reverse_p = jnp.exp(scores - lse[None, :])
        coupled = row_w[:, None] * toward + weights[None, :] * reverse_p
        coupled = coupled - (row_w[:, None] + weights[None, :]) * jnp.where(is_partner, 1.0, 0.0)
        weights_tile = jnp.where(on_diag, 0.0, coupled).astype(jnp.bfloat16)
        return jnp.dot(weights_tile, views, preferred_element_type=jnp.float32) * inv_temp
    dview = lax.map(backward, jnp.arange(block_count, dtype=jnp.int32)).reshape(total_rows, projections.shape[1])
    gradient = inv_norm * (dview - unit * lax.optimization_barrier(jnp.sum(unit * dview, axis=1, keepdims=True)))
    return (losses, gradient)
```

```python
import jax
import jax.numpy as jnp
from jax import lax
from jax.experimental import pallas as pl
from jax.experimental.pallas import tpu as pltpu
from jax.sharding import PartitionSpec as P

MESH = pl.DeviceIdType.MESH
inv_temp = 10.0
epsilon = 1e-06

SLOTS = (
    (2, 0, 1), (0, 2, 3), (1, 3, 3), (1, 2, 0), (3, 0, 1), (0, 0, 1),
    (0, 0, 3), (0, 3, 3), (1, 1, 0), (3, 0, 0), (0, 0, 0),
)
PARENT = (4, 7, 7, 8, 9, 10, 10, 10, 10, 10)
KIDS = ((0, 0), (0, 0), (0, 0), (0, 0), (0, 1), (0, 0), (0, 0), (1, 3), (3, 4), (4, 5), (5, 10))
SELF = 10
COUNT = 11
STEPS = (
    ((7, 10, 2, 8, 2), (9, 7, 2, 8, 2), (4, 7, 2, 6, 2), (10, 10, 2, 6, 2), (7, 5, 2, 1, 2),
     (9, 6, 2, 3, 1), (5, 8, 2, 1, 1), (2, 8, 2, 3, 2), (0, 5, 1, 6, 1)),
    ((10, 9, 2, 8, 2), (6, 8, 2, 5, 1), (2, 4, 2, 6, 2), (9, 5, 2, 2, 2), (4, 8, 2, 1, 2),
     (1, 9, 2, 6, 1), (3, 10, 2, 4, 2), (0, 10, 2, 8, 2), (0, 1, 1, 2, 2)),
)
NSTEP = 9
ZERO = 2 * NSTEP
CHUNKS = 3
RB = 32

NT = (((1,), (1,)), ((), ()))
NN = (((1,), (0,)), ((), ()))
TN = (((0,), (0,)), ((), ()))


def diff(a, b):
    return tuple((x - y) % 4 for x, y in zip(a, b))


def neg(a):
    return tuple(-x % 4 for x in a)


EDGE = tuple(diff(SLOTS[k], SLOTS[PARENT[k]]) for k in range(COUNT - 1))
PARTNERS = sorted(
    {d for s in SLOTS[:SELF] + EDGE for d in (s, neg(s))}
)


def backward_plan():
    out = []
    for steps in STEPS:
        prep, rows, cols, cols_a = [], [], [], []
        pb, rb, cb = [0], [0], [0]
        for k in range(COUNT):
            mine = []
            for t, (a, b1, _, b2, _) in enumerate(steps):
                if k in (a, b1, b2) and t not in prep:
                    prep.append(t)
                if a == k:
                    rows.append(t)
                for u, b in ((0, b1), (1, b2)):
                    if b == k and a != b:
                        mine.append((2 * t + u, a))
            if len(mine) % 2:
                mine.append((ZERO, SELF))
            for i in range(0, len(mine), 2):
                cols.append((mine[i][0], mine[i + 1][0], mine[i][1], mine[i + 1][1]))
            pb.append(len(prep))
            rb.append(len(rows))
            cb.append(len(cols))
        out.append((prep, rows, cols, pb, rb, cb))
    return out


PLAN = backward_plan()

UP_AFTER = (
    (), ((0, 0), (0, 1), (0, 2)), ((1, 0), (1, 1), (1, 2)), ((2, 0), (2, 1), (2, 2)),
    ((3, 0), (3, 1), (3, 2)), ((4, 0),), ((5, 0), (5, 1), (5, 2), (4, 1)),
    ((6, 0), (6, 1), (6, 2), (4, 2)), ((7, 0), (8, 0)), ((9, 0), (7, 1), (8, 1)),
    ((7, 2), (8, 2), (9, 1), (9, 2)),
)
UPS = tuple(e for l in UP_AFTER for e in l)
UP_BOUND = tuple(sum(len(l) for l in UP_AFTER[:i]) for i in range(COUNT + 1))


def lut(i, table):
    v = jnp.int32(table[0])
    for n in range(1, len(table)):
        v = jnp.where(i == n, jnp.int32(table[n]), v)
    return v


def lut2(i, c, t0, t1):
    n = max(len(t0), len(t1))
    t0 = tuple(t0) + (0,) * (n - len(t0))
    t1 = tuple(t1) + (0,) * (n - len(t1))
    if t0 == t1:
        return lut(i, t0)
    return lut(i, t0) * (1 - c) + lut(i, t1) * c


def kernel(
    x_ref, xw_ref, loss_ref, grad_ref,
    V, XT, XB, E, C, S, acc, H, TX, RX, RC, rsum, rpos, csum, cpos, SO, SI, SR, AO, AR, acol, wcol,
    gs, gr, ss, sr, us, ur, ts, tr, ms, mr, ps, pr, qs, qr,
):
    rows, width = x_ref.shape
    block = 2 * rows
    part = rows // CHUNKS
    grp = lax.axis_index("grp")
    dev = lax.axis_index("dev")
    c = grp % 2
    px, py, pz = (grp // 2) * 2 + dev // 16, (dev // 4) % 4, dev % 4

    def device(d, core):
        x, y, z = (px + d[0]) % 4, (py + d[1]) % 4, (pz + d[2]) % 4
        return ((x // 2) * 2 + core, (x % 2) * 16 + y * 4 + z)

    sibling = device((0, 0, 0), 1 - c)

    barrier = pltpu.get_barrier_semaphore()
    for d in PARTNERS:
        pl.semaphore_signal(barrier, inc=1, device_id=device(d, c), device_id_type=MESH)
    pl.semaphore_signal(barrier, inc=1, device_id=sibling, device_id_type=MESH)

    def base_of(k):
        x = (px + lut(k, [d[0] for d in SLOTS])) % 4
        y = (py + lut(k, [d[1] for d in SLOTS])) % 4
        z = (pz + lut(k, [d[2] for d in SLOTS])) % 4
        return ((x // 2) * 64 + (x % 2) * 16 + y * 4 + z) * rows

    own = pl.multiple_of(c * rows, 64)
    other = pl.multiple_of((1 - c) * rows, 64)

    def norm_body(i, _):
        r = pl.multiple_of(i * 32, 32)
        x = x_ref[pl.ds(r, 32), :]
        inv = lax.rsqrt(jnp.sum(x * x, axis=1, keepdims=True) + epsilon)
        V[SELF, pl.ds(pl.multiple_of(own + r, 32), 32), :] = (x * inv).astype(jnp.bfloat16)
        return 0

    lax.fori_loop(0, rows // 32, norm_body, 0)
    XT[SELF, c] = xw_ref[...]
    for ref in (rsum, rpos, csum, cpos):
        ref[...] = jnp.zeros_like(ref)

    pl.semaphore_wait(barrier, len(PARTNERS) + 1)

    def piece(k, j, core):
        if j == CHUNKS:
            return XT.at[k, core]
        r = pl.multiple_of(core * rows + j * part, 64)
        return V.at[k, pl.ds(r, part), :]

    def tree_copy(k, j):
        src, dst = piece(PARENT[k], j, c), piece(k, j, c)
        return pltpu.make_async_remote_copy(
            src_ref=src, dst_ref=dst, send_sem=gs.at[k, j], recv_sem=gr.at[k, j],
            device_id=device(neg(EDGE[k]), c), device_id_type=MESH,
        )

    def twin_copy(k, j):
        ref = piece(k, j, c)
        return pltpu.make_async_remote_copy(
            src_ref=ref, dst_ref=ref, send_sem=ss.at[k, j], recv_sem=sr.at[k, j],
            device_id=sibling, device_id_type=MESH,
        )

    def arrive(k, j):
        tree_copy(k, j).wait_recv()
        for child in range(*KIDS[k]):
            tree_copy(child, j).start()
        twin_copy(k, j).start()

    def twins(k):
        for j in range(CHUNKS + 1):
            twin_copy(k, j).wait_recv()
        XB[k] = XT[k, 0] + XT[k, 1]

    for k in (9, 8, 7, 6, 5):
        tree_copy(k, CHUNKS).start()
    for j in range(CHUNKS):
        for k in (9, 8, 7):
            tree_copy(k, j).start()
        if j == 0:
            tree_copy(5, 0).start()
    for j in range(CHUNKS + 1):
        twin_copy(SELF, j).start()

    def gate0():
        for k in (9, 8, 7):
            arrive(k, CHUNKS)
        for j in range(CHUNKS):
            arrive(9, j)
            if j + 1 < CHUNKS:
                tree_copy(5, j + 1).start()
            arrive(8, j)
            arrive(7, j)
            tree_copy(6, j).start()
        for k in (SELF, 9, 8, 7):
            twins(k)

    def gate1():
        for k in (5, 6, 4):
            arrive(k, CHUNKS)
        for j in range(CHUNKS):
            arrive(4, j)
            arrive(5, j)
        for j in range(CHUNKS):
            arrive(6, j)
        for k in (5, 4, 6):
            twins(k)

    def gate2():
        for k in (3, 2, 1):
            arrive(k, CHUNKS)
        for j in range(CHUNKS):
            for k in (3, 2, 1):
                arrive(k, j)
        for k in (3, 2, 1):
            twins(k)

    def gate3():
        for j in (CHUNKS,) + tuple(range(CHUNKS)):
            arrive(0, j)
        twins(0)

    def step_of(t):
        cols = [[[s[n] for s in STEPS[core]] for n in range(5)] for core in (0, 1)]
        a, b1, h1, b2, h2 = (lut2(t, c, cols[0][n], cols[1][n]) for n in range(5))
        return a, b1, h1.astype(jnp.float32) * 0.5, b2, h2.astype(jnp.float32) * 0.5

    lane = lax.broadcasted_iota(jnp.int32, (1, block), 1)
    sub_row = lax.broadcasted_iota(jnp.int32, (RB, 1), 0)
    far = 32 * rows - rows

    def tile_rows(t):
        a, b1, h1, b2, h2 = step_of(t)
        partner = jnp.concatenate([XB[b1, 1:2, :], XB[b2, 1:2, :]], axis=1)
        weight = jnp.concatenate(
            [jnp.full((1, block), h1, jnp.float32), jnp.full((1, block), h2, jnp.float32)], axis=1
        )
        return a, b1, b2, partner, weight

    def row_ids(a, r):
        start = base_of(a) + r + jnp.where(r >= rows, far, 0)
        return (start + sub_row).astype(jnp.float32)

    def column_ids(b):
        return (base_of(b) + lane + jnp.where(lane >= rows, far, 0)).astype(jnp.float32)

    def score_step(t, _):
        for n, gate in ((0, gate0), (1, gate1), (2, gate2), (7, gate3)):
            pl.when(t == n)(gate)
        a, b1, b2, partner, weight = tile_rows(t)
        S[...] = lax.dot_general(
            V[a], jnp.concatenate([V[b1], V[b2]], axis=0), NT, preferred_element_type=jnp.float32
        )
        ids = jnp.concatenate([column_ids(b1), column_ids(b2)], axis=1)

        def rows_body(i, carry):
            es, ps_ = carry
            r = pl.multiple_of(i * RB, RB)
            s = S[pl.ds(r, RB), :] * inv_temp
            rid = row_ids(a, r)
            e = jnp.exp(s - inv_temp) * weight
            e = jnp.where(rid == ids, 0.0, e)
            m = jnp.where(rid == partner, s * weight, 0.0)
            E[t, pl.ds(r, RB), :] = e
            er, mr_ = e[:, :128], m[:, :128]
            for n in range(1, 2 * block // 128):
                er = er + e[:, n * 128 : (n + 1) * 128]
                mr_ = mr_ + m[:, n * 128 : (n + 1) * 128]
            rsum[a, pl.ds(r, RB), :] += er
            rpos[a, pl.ds(r, RB), :] += mr_
            for n in range(RB // 8):
                es = es + e[n * 8 : (n + 1) * 8, :]
                ps_ = ps_ + m[n * 8 : (n + 1) * 8, :]
            return es, ps_

        zero = jnp.zeros((8, 2 * block), jnp.float32)
        es, ps_ = lax.fori_loop(0, block // RB, rows_body, (zero, zero))
        for n, b in ((0, b1), (1, b2)):
            use = jnp.where(a == b, 0.0, 1.0)
            csum[b] += es[:, n * block : (n + 1) * block] * use
            cpos[b] += ps_[:, n * block : (n + 1) * block] * use
        return 0

    lax.fori_loop(0, NSTEP, score_step, 0)

    def total(rs, cs):
        return jnp.sum(rs.T, axis=0, keepdims=True) + jnp.sum(cs, axis=0, keepdims=True)

    def sums_body(k, _):
        SO[k, 0:1, :] = total(rsum[k], csum[k])
        SO[k, 1:2, :] = total(rpos[k], cpos[k])
        return 0

    SO[...] = jnp.zeros_like(SO)
    lax.fori_loop(0, COUNT, sums_body, 0)

    twin_sums = pltpu.make_async_remote_copy(
        src_ref=SO, dst_ref=SI, send_sem=ms, recv_sem=mr, device_id=sibling, device_id_type=MESH
    )
    twin_sums.start()

    def wide(row):
        return jnp.broadcast_to(row, (128, block)).T

    def wcol_body(k, _):
        wcol[k] = wide(XB[k, 0:1, :])
        return 0

    lax.fori_loop(0, COUNT, wcol_body, 0)
    twin_sums.wait()
    SI[...] = SO[...] + SI[...]

    def sum_copy(k):
        return pltpu.make_async_remote_copy(
            src_ref=SI.at[k], dst_ref=SR.at[k], send_sem=ps.at[k], recv_sem=pr.at[k],
            device_id=device(SLOTS[k], c), device_id_type=MESH,
        )

    def scale_copy(k):
        return pltpu.make_async_remote_copy(
            src_ref=AO, dst_ref=AR.at[k], send_sem=qs.at[k], recv_sem=qr.at[k],
            device_id=device(neg(SLOTS[k]), c), device_id_type=MESH,
        )

    for k in range(COUNT - 1):
        sum_copy(k).start()
    both = SI[SELF]
    for k in range(COUNT - 1):
        sum_copy(k).wait_recv()
        both = both + SR[k]
    exp_sum, positive = both[0:1, :], both[1:2, :]
    scale = XB[SELF, 0:1, :] / exp_sum
    AO[...] = jnp.broadcast_to(scale, (8, block))
    for k in range(COUNT - 1):
        scale_copy(k).start()
    AR[SELF] = AO[...]
    losses = jnp.broadcast_to(inv_temp + jnp.log(exp_sum) - positive, (8, block))
    loss_ref[...] = jnp.where(c == 0, losses, pltpu.roll(losses, rows, 1))
    C[ZERO] = jnp.zeros((block, block), jnp.bfloat16)
    for k in range(COUNT - 1):
        scale_copy(k).wait_recv()

    def acol_body(k, _):
        acol[k] = wide(AR[k, 0:1, :])
        return 0

    lax.fori_loop(0, COUNT, acol_body, 0)

    def twin_part(k):
        return pltpu.make_async_remote_copy(
            src_ref=TX.at[k], dst_ref=RX.at[k], send_sem=ts.at[k], recv_sem=tr.at[k],
            device_id=sibling, device_id_type=MESH,
        )

    def up_copy(k, j, d):
        r = pl.multiple_of(j * part, 64)
        return pltpu.make_async_remote_copy(
            src_ref=TX.at[k, pl.ds(r, part), :], dst_ref=RC.at[k, pl.ds(r, part), :],
            send_sem=us.at[k, j], recv_sem=ur.at[k, j], device_id=device(d, c), device_id_type=MESH,
        )

    def edge_of(k):
        return tuple(lut(k, [e[n] for e in EDGE]) for n in range(3))

    def gathered(k, j, lo, hi):
        r = pl.multiple_of(j * part, 64)

        def child(n, _):
            up_copy(n, j, (0, 0, 1)).wait_recv()
            H[k, pl.ds(r, part), :] += RC[n, pl.ds(r, part), :].astype(jnp.float32)
            return 0

        lax.fori_loop(lo, hi, child, 0)

    def up_event(ev, _):
        k = lut(ev, [e[0] for e in UPS])
        j = lut(ev, [e[1] for e in UPS])

        @pl.when(j == 0)
        def _():
            twin_part(k).wait()

        gathered(k, j, lut(k, [a for a, _ in KIDS]), lut(k, [b for _, b in KIDS]))
        r = pl.multiple_of(j * part, 64)
        TX[k, pl.ds(r, part), :] = (
            H[k, pl.ds(r, part), :] + RX[k, pl.ds(r, part), :].astype(jnp.float32)
        ).astype(jnp.bfloat16)
        up_copy(k, j, edge_of(k)).start()
        return 0

    def prepare(n, _):
        t = lut2(n, c, PLAN[0][0], PLAN[1][0])
        a, b1, b2, partner, weight = tile_rows(t)
        arow = jnp.concatenate([AR[b1, 0:1, :], AR[b2, 0:1, :]], axis=1)
        wrow = jnp.concatenate([XB[b1, 0:1, :], XB[b2, 0:1, :]], axis=1)

        def rows_body(i, _):
            r = pl.multiple_of(i * RB, RB)
            rid = row_ids(a, r)
            ac, wc = acol[a, pl.ds(r, RB), :], wcol[a, pl.ds(r, RB), :]
            ac = jnp.concatenate([ac] * (2 * block // 128), axis=1)
            wc = jnp.concatenate([wc] * (2 * block // 128), axis=1)
            v = E[t, pl.ds(r, RB), :] * (ac + arow)
            v = (v - jnp.where(rid == partner, (wc + wrow) * weight, 0.0)).astype(jnp.bfloat16)
            C[2 * t, pl.ds(r, RB), :] = v[:, :block]
            C[2 * t + 1, pl.ds(r, RB), :] = v[:, block:]
            return 0

        lax.fori_loop(0, block // RB, rows_body, 0)
        return 0

    def row_product(n, _):
        t = lut2(n, c, PLAN[0][1], PLAN[1][1])
        _, b1, _, b2, _ = step_of(t)
        acc[...] += lax.dot_general(
            jnp.concatenate([C[2 * t], C[2 * t + 1]], axis=1),
            jnp.concatenate([V[b1], V[b2]], axis=0),
            NN, preferred_element_type=jnp.float32,
        )
        return 0

    def column_product(n, _):
        u1, u2, a1, a2 = (
            lut2(n, c, [q[i] for q in PLAN[0][2]], [q[i] for q in PLAN[1][2]]) for i in range(4)
        )
        acc[...] += lax.dot_general(
            jnp.concatenate([C[u1], C[u2]], axis=0),
            jnp.concatenate([V[a1], V[a2]], axis=0),
            TN, preferred_element_type=jnp.float32,
        )
        return 0

    def slot_body(k, _):
        for n, body in ((3, prepare), (4, row_product), (5, column_product)):
            if n == 4:
                acc[...] = jnp.zeros_like(acc)
            lo = lut2(k, c, PLAN[0][n][:-1], PLAN[1][n][:-1])
            hi = lut2(k, c, PLAN[0][n][1:], PLAN[1][n][1:])
            lax.fori_loop(lo, hi, body, 0)
        H[k] = acc[pl.ds(own, rows), :]
        TX[k] = acc[pl.ds(other, rows), :].astype(jnp.bfloat16)
        twin_part(k).start()
        lax.fori_loop(lut(k, UP_BOUND[:-1]), lut(k, UP_BOUND[1:]), up_event, 0)
        return 0

    lax.fori_loop(0, COUNT, slot_body, 0)

    twin_part(SELF).wait()

    def finish(j, _):
        gathered(SELF, j, *KIDS[SELF])

        def body(i, _):
            r = pl.multiple_of(j * part + i * 16, 16)
            x = x_ref[pl.ds(r, 16), :]
            inv = lax.rsqrt(jnp.sum(x * x, axis=1, keepdims=True) + epsilon)
            unit = x * inv
            dview = (H[SELF, pl.ds(r, 16), :] + RX[SELF, pl.ds(r, 16), :].astype(jnp.float32)) * inv_temp
            grad_ref[pl.ds(r, 16), :] = inv * (
                dview - unit * jnp.sum(unit * dview, axis=1, keepdims=True)
            )
            return 0

        lax.fori_loop(0, part // 16, body, 0)
        return 0

    lax.fori_loop(0, CHUNKS, finish, 0)

    for k in range(COUNT - 1):
        for j in range(CHUNKS + 1):
            tree_copy(k, j).wait_send()
        for j in range(CHUNKS):
            up_copy(k, j, EDGE[k]).wait_send()
        sum_copy(k).wait_send()
        scale_copy(k).wait_send()
    for k in range(COUNT):
        for j in range(CHUNKS + 1):
            twin_copy(k, j).wait_send()


def local(projections, row_weights, partner):
    rows, width = projections.shape
    block = 2 * rows
    core = lax.axis_index("grp") % 2
    mine = jnp.stack([row_weights.astype(jnp.float32), partner.astype(jnp.float32)])
    mine = jnp.pad(mine, ((0, 6), (0, 0)))
    none = jnp.zeros_like(mine)
    extras = jnp.where(
        core == 0, jnp.concatenate([mine, none], 1), jnp.concatenate([none, mine], 1)
    )
    f32, bf16 = jnp.float32, jnp.bfloat16
    vm, dma = pltpu.VMEM, pltpu.SemaphoreType.DMA
    losses, gradient = pl.pallas_call(
        kernel,
        out_shape=(
            jax.ShapeDtypeStruct((8, block), f32),
            jax.ShapeDtypeStruct((rows, width), f32),
        ),
        in_specs=[pl.BlockSpec(memory_space=vm)] * 2,
        out_specs=[pl.BlockSpec(memory_space=vm)] * 2,
        scratch_shapes=[
            vm((COUNT, block, width), bf16),
            vm((COUNT, 2, 8, block), f32),
            vm((COUNT, 8, block), f32),
            vm((NSTEP, block, 2 * block), f32),
            vm((2 * NSTEP + 1, block, block), bf16),
            vm((block, 2 * block), f32),
            vm((block, width), f32),
            vm((COUNT, rows, width), f32),
            vm((COUNT, rows, width), bf16),
            vm((COUNT, rows, width), bf16),
            vm((COUNT - 1, rows, width), bf16),
            vm((COUNT, block, 128), f32),
            vm((COUNT, block, 128), f32),
            vm((COUNT, 8, block), f32),
            vm((COUNT, 8, block), f32),
            vm((COUNT, 8, block), f32),
            vm((COUNT, 8, block), f32),
            vm((COUNT - 1, 8, block), f32),
            vm((8, block), f32),
            vm((COUNT, 8, block), f32),
            vm((COUNT, block, 128), f32),
            vm((COUNT, block, 128), f32),
            dma((COUNT - 1, CHUNKS + 1)), dma((COUNT - 1, CHUNKS + 1)),
            dma((COUNT, CHUNKS + 1)), dma((COUNT, CHUNKS + 1)),
            dma((COUNT - 1, CHUNKS)), dma((COUNT - 1, CHUNKS)),
            dma((COUNT,)), dma((COUNT,)),
            dma, dma,
            dma((COUNT - 1,)), dma((COUNT - 1,)),
            dma((COUNT - 1,)), dma((COUNT - 1,)),
        ],
        compiler_params=pltpu.CompilerParams(
            collective_id=0, has_side_effects=True, vmem_limit_bytes=63 * 2**20
        ),
        cost_estimate=pl.CostEstimate(
            flops=16 * 10**9, bytes_accessed=2 * 10**6, transcendentals=3 * 10**6
        ),
    )(projections, extras)
    return losses[0, :rows], gradient


def solution(mesh):
    return jax.shard_map(
        local,
        mesh=mesh,
        in_specs=(P(("grp", "dev"), None), P(("grp", "dev")), P(("grp", "dev"))),
        out_specs=(P(("grp", "dev")), P(("grp", "dev"), None)),
        check_vma=False,
    )
```

```python
import jax
import jax.numpy as jnp
from jax import lax
from jax.experimental import pallas as pl
from jax.experimental.pallas import tpu as pltpu
from jax.sharding import PartitionSpec as P

MESH = pl.DeviceIdType.MESH
inv_temp = 10.0
epsilon = 1e-06

SLOTS = (
    (2, 0, 1), (0, 2, 3), (1, 3, 3), (1, 2, 0), (3, 0, 1), (0, 0, 1),
    (0, 0, 3), (0, 3, 3), (1, 1, 0), (3, 0, 0), (0, 0, 0),
)
PARENT = (4, 7, 7, 8, 9, 10, 10, 10, 10, 10)
KIDS = ((0, 0), (0, 0), (0, 0), (0, 0), (0, 1), (0, 0), (0, 0), (1, 3), (3, 4), (4, 5), (5, 10))
SELF = 10
COUNT = 11
STEPS = (
    ((10, 10, 2, 7, 2), (8, 9, 2, 5, 2), (9, 7, 2, 5, 2), (2, 5, 2, 4, 2), (3, 10, 2, 8, 2),
     (6, 8, 2, 5, 1), (8, 2, 2, 1, 2), (1, 9, 2, 4, 2), (0, 2, 2, 1, 1)),
    ((10, 8, 2, 5, 2), (4, 10, 2, 8, 2), (2, 7, 2, 3, 2), (9, 2, 2, 3, 1), (6, 2, 2, 4, 2),
     (5, 7, 2, 1, 1), (3, 4, 2, 0, 2), (0, 10, 2, 5, 1), (6, 1, 1, 0, 1)),
)
NSTEP = 9
ROUNDS = (
    ((9, 0), (7, 0), (8, 0), (5, 0), (9, 1), (7, 1), (8, 1), (5, 1), (9, 2), (7, 2), (8, 2), (5, 2)),
    (),
    ((4, 0), (2, 0), (3, 0), (6, 0), (1, 0)),
    ((4, 1), (2, 1), (3, 1), (6, 1), (1, 1)),
    ((4, 2), (0, 0), (2, 2), (3, 2), (6, 2), (1, 2)),
    (),
    ((0, 1),),
    (),
    ((0, 2),),
    (), (), (), (),
)
ROUND_STEP = (
    (0, 1, 2, -1, 3, 4, 5, 6, 7, 8, -1, -1, -1),
    (0, -1, -1, -1, 1, 2, 3, 4, 5, 6, 7, 8, -1),
)
ZERO = 2 * NSTEP
CHUNKS = 3
RB = 96

NT = (((1,), (1,)), ((), ()))
NN = (((1,), (0,)), ((), ()))
TN = (((0,), (0,)), ((), ()))


def diff(a, b):
    return tuple((x - y) % 4 for x, y in zip(a, b))


def neg(a):
    return tuple(-x % 4 for x in a)


EDGE = tuple(diff(SLOTS[k], SLOTS[PARENT[k]]) for k in range(COUNT - 1))
GREET = tuple(sorted(set(EDGE)))


ORDER = (4, 9, 6, 0, 2, 3, 1, 7, 5, 8, 10)


def backward_plan():
    out = []
    for steps in STEPS:
        prep, rows, cols, cols_a = [], [], [], []
        pb, rb, cb = [0], [0], [0]
        for k in ORDER:
            mine = []
            for t, (a, b1, _, b2, _) in enumerate(steps):
                if k in (a, b1, b2) and t not in prep:
                    prep.append(t)
                if a == k:
                    rows.append(t)
                for u, b in ((0, b1), (1, b2)):
                    if b == k and a != b:
                        mine.append((2 * t + u, a))
            if len(mine) % 2:
                mine.append((ZERO, SELF))
            for i in range(0, len(mine), 2):
                cols.append((mine[i][0], mine[i + 1][0], mine[i][1], mine[i + 1][1]))
            pb.append(len(prep))
            rb.append(len(rows))
            cb.append(len(cols))
        out.append((prep, rows, cols, pb, rb, cb))
    return out


PLAN = backward_plan()

UP_AFTER = (
    (),
    (),
    (),
    ((6, 0), (6, 1), (6, 2)),
    ((0, 0), (0, 1), (0, 2)),
    ((2, 0), (2, 1), (2, 2)),
    ((3, 0), (4, 0), (3, 1), (3, 2)),
    ((1, 0), (1, 1), (4, 1), (1, 2)),
    ((4, 2), (9, 0)),
    ((7, 0), (9, 1), (5, 0), (5, 1), (5, 2), (7, 1), (8, 0), (8, 1), (8, 2), (9, 2)),
    ((7, 2),),
)
UPS = tuple(e for l in UP_AFTER for e in l)
UP_BOUND = tuple(sum(len(l) for l in UP_AFTER[:i]) for i in range(COUNT + 1))


def lut(i, table):
    v = jnp.int32(table[0])
    for n in range(1, len(table)):
        v = jnp.where(i == n, jnp.int32(table[n]), v)
    return v


def lut2(i, c, t0, t1):
    n = max(len(t0), len(t1))
    t0 = tuple(t0) + (0,) * (n - len(t0))
    t1 = tuple(t1) + (0,) * (n - len(t1))
    if t0 == t1:
        return lut(i, t0)
    return lut(i, t0) * (1 - c) + lut(i, t1) * c


def kernel(
    x_ref, xw_ref, loss_ref, grad_ref,
    V, XT, XB, E, C, S, acc, H, TX, RX, RC, rsum, rpos, csum, cpos, SO, SI, SR, AO, AR, acol, wcol,
    gs, gr, ss, sr, us, ur, ts, tr, ms, mr, ps, pr, qs, qr,
):
    rows, width = x_ref.shape
    block = 2 * rows
    part = rows // CHUNKS
    grp = lax.axis_index("grp")
    dev = lax.axis_index("dev")
    c = grp % 2
    px, py, pz = (grp // 2) * 2 + dev // 16, (dev // 4) % 4, dev % 4

    def device(d, core):
        x, y, z = (px + d[0]) % 4, (py + d[1]) % 4, (pz + d[2]) % 4
        return ((x // 2) * 2 + core, (x % 2) * 16 + y * 4 + z)

    sibling = device((0, 0, 0), 1 - c)

    barrier = pltpu.get_barrier_semaphore()
    for d in GREET:
        pl.semaphore_signal(barrier, inc=1, device_id=device(d, c), device_id_type=MESH)
    pl.semaphore_signal(barrier, inc=1, device_id=sibling, device_id_type=MESH)

    def base_of(k):
        x = (px + lut(k, [d[0] for d in SLOTS])) % 4
        y = (py + lut(k, [d[1] for d in SLOTS])) % 4
        z = (pz + lut(k, [d[2] for d in SLOTS])) % 4
        return ((x // 2) * 64 + (x % 2) * 16 + y * 4 + z) * rows

    own = pl.multiple_of(c * rows, 64)
    other = pl.multiple_of((1 - c) * rows, 64)

    def norm_body(i, _):
        r = pl.multiple_of(i * 32, 32)
        x = x_ref[pl.ds(r, 32), :]
        inv = lax.rsqrt(jnp.sum(x * x, axis=1, keepdims=True) + epsilon)
        V[SELF, pl.ds(pl.multiple_of(own + r, 32), 32), :] = (x * inv).astype(jnp.bfloat16)
        return 0

    lax.fori_loop(0, rows // 32, norm_body, 0)
    XT[SELF, c] = xw_ref[...]
    for ref in (rsum, rpos, csum, cpos):
        ref[...] = jnp.zeros_like(ref)

    pl.semaphore_wait(barrier, len(GREET) + 1)

    def piece(k, j, core):
        if j == CHUNKS:
            return XT.at[k, core]
        r = pl.multiple_of(core * rows + j * part, 64)
        return V.at[k, pl.ds(r, part), :]

    def tree_copy(k, j):
        src, dst = piece(PARENT[k], j, c), piece(k, j, c)
        return pltpu.make_async_remote_copy(
            src_ref=src, dst_ref=dst, send_sem=gs.at[k, j], recv_sem=gr.at[k, j],
            device_id=device(neg(EDGE[k]), c), device_id_type=MESH,
        )

    def twin_copy(k, j):
        ref = piece(k, j, c)
        return pltpu.make_async_remote_copy(
            src_ref=ref, dst_ref=ref, send_sem=ss.at[k, j], recv_sem=sr.at[k, j],
            device_id=sibling, device_id_type=MESH,
        )

    def arrive(k, j):
        tree_copy(k, j).wait_recv()
        for child in range(*KIDS[k]):
            tree_copy(child, j).start()
        twin_copy(k, j).start()

    def twins(k):
        for j in range(CHUNKS + 1):
            twin_copy(k, j).wait_recv()
        XB[k] = XT[k, 0] + XT[k, 1]

    for k in (9, 8, 7, 5, 6):
        tree_copy(k, CHUNKS).start()
    for j in range(CHUNKS):
        for k in (9, 8, 7, 5):
            tree_copy(k, j).start()
    for j in range(CHUNKS):
        tree_copy(6, j).start()
    for j in range(CHUNKS + 1):
        twin_copy(SELF, j).start()

    def gate(events):
        for k, j in events:
            if j == 0:
                arrive(k, CHUNKS)
            arrive(k, j)
        for k, j in events:
            if j == CHUNKS - 1:
                twins(k)

    def step_of(t):
        cols = [[[s[n] for s in STEPS[core]] for n in range(5)] for core in (0, 1)]
        a, b1, h1, b2, h2 = (lut2(t, c, cols[0][n], cols[1][n]) for n in range(5))
        return a, b1, h1.astype(jnp.float32) * 0.5, b2, h2.astype(jnp.float32) * 0.5

    lane = lax.broadcasted_iota(jnp.int32, (1, block), 1)
    sub_row = lax.broadcasted_iota(jnp.int32, (RB, 1), 0)
    far = 32 * rows - rows

    def tile_rows(t):
        a, b1, h1, b2, h2 = step_of(t)
        partner = jnp.concatenate([XB[b1, 1:2, :], XB[b2, 1:2, :]], axis=1)
        weight = jnp.concatenate(
            [jnp.full((1, block), h1, jnp.float32), jnp.full((1, block), h2, jnp.float32)], axis=1
        )
        return a, b1, b2, partner, weight

    def row_ids(a, r):
        start = base_of(a) + r + jnp.where(r >= rows, far, 0)
        return (start + sub_row).astype(jnp.float32)

    def column_ids(b):
        return (base_of(b) + lane + jnp.where(lane >= rows, far, 0)).astype(jnp.float32)

    def score_round(n, _):
        for m, events in enumerate(ROUNDS):
            if events:
                @pl.when(n == m)
                def _(events=events):
                    gate(events)
                    if events == ROUNDS[0]:
                        twins(SELF)
        t = lut2(n, c, ROUND_STEP[0], ROUND_STEP[1])
        pl.when(t >= 0)(lambda: score_step(t))
        return 0

    def score_step(t):
        a, b1, b2, partner, weight = tile_rows(t)
        S[...] = lax.dot_general(
            V[a], jnp.concatenate([V[b1], V[b2]], axis=0), NT, preferred_element_type=jnp.float32
        )
        ids = jnp.concatenate([column_ids(b1), column_ids(b2)], axis=1)

        offset = inv_temp - jnp.log(weight)
        half1, half2 = weight[0:1, 0:128], weight[0:1, block : block + 128]

        def rows_body(i, carry):
            es, ps_ = carry
            r = pl.multiple_of(i * RB, RB)
            s = S[pl.ds(r, RB), :]
            rid = row_ids(a, r)
            e = jnp.where(rid == ids, 0.0, jnp.exp(s * inv_temp - offset))
            m = jnp.where(rid == partner, s, 0.0)
            E[t, pl.ds(r, RB), :] = e
            er = [e[:, n * 128 : (n + 1) * 128] for n in range(6)]
            mr_ = [m[:, n * 128 : (n + 1) * 128] for n in range(6)]
            rsum[a, pl.ds(r, RB), :] += er[0] + er[1] + er[2] + er[3] + er[4] + er[5]
            rpos[a, pl.ds(r, RB), :] += (mr_[0] + mr_[1] + mr_[2]) * half1 + (mr_[3] + mr_[4] + mr_[5]) * half2
            for n in range(RB // 8):
                es = es + e[n * 8 : (n + 1) * 8, :]
                ps_ = ps_ + m[n * 8 : (n + 1) * 8, :]
            return es, ps_

        zero = jnp.zeros((8, 2 * block), jnp.float32)
        es, ps_ = lax.fori_loop(0, block // RB, rows_body, (zero, zero))
        ps_ = ps_ * weight
        for n, b in ((0, b1), (1, b2)):
            use = jnp.where(a == b, 0.0, 1.0)
            csum[b] += es[:, n * block : (n + 1) * block] * use
            cpos[b] += ps_[:, n * block : (n + 1) * block] * use

    lax.fori_loop(0, 12, score_round, 0)

    def total(rs, cs):
        return jnp.sum(rs.T, axis=0, keepdims=True) + jnp.sum(cs, axis=0, keepdims=True)

    def sums_of(k):
        SO[k] = jnp.concatenate(
            [total(rsum[k], csum[k]), total(rpos[k], cpos[k]), jnp.zeros((6, block), jnp.float32)], axis=0
        )

    def sum_copy(k):
        return pltpu.make_async_remote_copy(
            src_ref=SO.at[k], dst_ref=SR.at[k], send_sem=ps.at[k], recv_sem=pr.at[k],
            device_id=device(SLOTS[k], c), device_id_type=MESH,
        )

    def scale_copy(k):
        return pltpu.make_async_remote_copy(
            src_ref=AO, dst_ref=AR.at[k], send_sem=qs.at[k], recv_sem=qr.at[k],
            device_id=device(neg(SLOTS[k]), c), device_id_type=MESH,
        )

    for k in range(COUNT - 1):
        sums_of(k)
        sum_copy(k).start()
    sums_of(SELF)

    def wide(row):
        return jnp.broadcast_to(row, (128, block)).T

    def wcol_body(k, _):
        wcol[k] = wide(XB[k, 0:1, :])
        return 0

    lax.fori_loop(0, COUNT, wcol_body, 0)
    C[ZERO] = jnp.zeros((block, block), jnp.bfloat16)
    acc[...] = jnp.zeros_like(acc)
    mine = SO[SELF]
    for k in range(COUNT - 1):
        sum_copy(k).wait_recv()
        mine = mine + SR[k]
    SI[0] = mine
    twin_sums = pltpu.make_async_remote_copy(
        src_ref=SI.at[0], dst_ref=SI.at[1], send_sem=ms, recv_sem=mr, device_id=sibling, device_id_type=MESH
    )
    twin_sums.start()
    twin_sums.wait()
    both = SI[0] + SI[1]
    exp_sum, positive = both[0:1, :], both[1:2, :] * inv_temp
    scale = XB[SELF, 0:1, :] / exp_sum
    AO[...] = jnp.broadcast_to(scale, (8, block))
    for k in range(COUNT - 1):
        scale_copy(k).start()
    AR[SELF] = AO[...]
    losses = jnp.broadcast_to(inv_temp + jnp.log(exp_sum) - positive, (8, block))
    loss_ref[...] = jnp.where(c == 0, losses, pltpu.roll(losses, rows, 1))[0:1, :rows]
    for k in range(COUNT - 1):
        scale_copy(k).wait_recv()

    def twin_part(k):
        return pltpu.make_async_remote_copy(
            src_ref=TX.at[k], dst_ref=RX.at[k], send_sem=ts.at[k], recv_sem=tr.at[k],
            device_id=sibling, device_id_type=MESH,
        )

    def up_copy(k, j, d):
        r = pl.multiple_of(j * part, 64)
        return pltpu.make_async_remote_copy(
            src_ref=TX.at[k, pl.ds(r, part), :], dst_ref=RC.at[k, pl.ds(r, part), :],
            send_sem=us.at[k, j], recv_sem=ur.at[k, j], device_id=device(d, c), device_id_type=MESH,
        )

    def edge_of(k):
        return tuple(lut(k, [e[n] for e in EDGE]) for n in range(3))

    def gathered(k, j, lo, hi):
        r = pl.multiple_of(j * part, 64)

        def child(n, _):
            up_copy(n, j, (0, 0, 1)).wait_recv()
            H[k, pl.ds(r, part), :] += RC[n, pl.ds(r, part), :].astype(jnp.float32)
            return 0

        lax.fori_loop(lo, hi, child, 0)

    def up_event(ev, _):
        k = lut(ev, [e[0] for e in UPS])
        j = lut(ev, [e[1] for e in UPS])

        @pl.when(j == 0)
        def _():
            twin_part(k).wait()

        gathered(k, j, lut(k, [a for a, _ in KIDS]), lut(k, [b for _, b in KIDS]))
        r = pl.multiple_of(j * part, 64)
        TX[k, pl.ds(r, part), :] = (
            H[k, pl.ds(r, part), :] + RX[k, pl.ds(r, part), :].astype(jnp.float32)
        ).astype(jnp.bfloat16)
        up_copy(k, j, edge_of(k)).start()
        return 0

    def prepare(n, _):
        t = lut2(n, c, PLAN[0][0], PLAN[1][0])
        a, b1, b2, partner, weight = tile_rows(t)
        acol[...] = wide(AR[a, 0:1, :])
        arow = jnp.concatenate([AR[b1, 0:1, :], AR[b2, 0:1, :]], axis=1)
        wrow = jnp.concatenate([XB[b1, 0:1, :], XB[b2, 0:1, :]], axis=1)

        def rows_body(i, _):
            r = pl.multiple_of(i * RB, RB)
            rid = row_ids(a, r)
            ac, wc = acol[pl.ds(r, RB), :], wcol[a, pl.ds(r, RB), :]
            ac = jnp.concatenate([ac] * (2 * block // 128), axis=1)
            wc = jnp.concatenate([wc] * (2 * block // 128), axis=1)
            v = E[t, pl.ds(r, RB), :] * (ac + arow)
            v = (v - jnp.where(rid == partner, (wc + wrow) * weight, 0.0)).astype(jnp.bfloat16)
            C[2 * t, pl.ds(r, RB), :] = v[:, :block]
            C[2 * t + 1, pl.ds(r, RB), :] = v[:, block:]
            return 0

        lax.fori_loop(0, block // RB, rows_body, 0)
        return 0

    def row_product(n, _):
        t = lut2(n, c, PLAN[0][1], PLAN[1][1])
        _, b1, _, b2, _ = step_of(t)
        acc[...] += lax.dot_general(
            jnp.concatenate([C[2 * t], C[2 * t + 1]], axis=1),
            jnp.concatenate([V[b1], V[b2]], axis=0),
            NN, preferred_element_type=jnp.float32,
        )
        return 0

    def column_product(n, _):
        u1, u2, a1, a2 = (
            lut2(n, c, [q[i] for q in PLAN[0][2]], [q[i] for q in PLAN[1][2]]) for i in range(4)
        )
        acc[...] += lax.dot_general(
            jnp.concatenate([C[u1], C[u2]], axis=0),
            jnp.concatenate([V[a1], V[a2]], axis=0),
            TN, preferred_element_type=jnp.float32,
        )
        return 0

    def slot_body(i, _):
        k = lut(i, ORDER)
        for n, body in ((3, prepare), (4, row_product), (5, column_product)):
            lo = lut2(i, c, PLAN[0][n][:-1], PLAN[1][n][:-1])
            hi = lut2(i, c, PLAN[0][n][1:], PLAN[1][n][1:])
            lax.fori_loop(lo, hi, body, 0)

        def split(n, _):
            r = pl.multiple_of(n * 32, 32)
            theirs = pl.ds(pl.multiple_of(other + r, 32), 32)
            ours = pl.ds(pl.multiple_of(own + r, 32), 32)
            TX[k, pl.ds(r, 32), :] = acc[theirs, :].astype(jnp.bfloat16)
            H[k, pl.ds(r, 32), :] = acc[ours, :]
            zero = jnp.zeros((32, width), jnp.float32)
            acc[theirs, :] = zero
            acc[ours, :] = zero
            return 0

        lax.fori_loop(0, rows // 32, split, 0)
        twin_part(k).start()
        lax.fori_loop(lut(i, UP_BOUND[:-1]), lut(i, UP_BOUND[1:]), up_event, 0)
        return 0

    lax.fori_loop(0, COUNT, slot_body, 0)

    twin_part(SELF).wait()

    def finish(j, _):
        gathered(SELF, j, *KIDS[SELF])

        def body(i, _):
            r = pl.multiple_of(j * part + i * 16, 16)
            x = x_ref[pl.ds(r, 16), :]
            inv = lax.rsqrt(jnp.sum(x * x, axis=1, keepdims=True) + epsilon)
            unit = x * inv
            dview = (H[SELF, pl.ds(r, 16), :] + RX[SELF, pl.ds(r, 16), :].astype(jnp.float32)) * inv_temp
            grad_ref[pl.ds(r, 16), :] = inv * (
                dview - unit * jnp.sum(unit * dview, axis=1, keepdims=True)
            )
            return 0

        lax.fori_loop(0, part // 16, body, 0)
        return 0

    lax.fori_loop(0, CHUNKS, finish, 0)

    for k in range(COUNT - 1):
        for j in range(CHUNKS + 1):
            tree_copy(k, j).wait_send()
        for j in range(CHUNKS):
            up_copy(k, j, EDGE[k]).wait_send()
        sum_copy(k).wait_send()
        scale_copy(k).wait_send()
    for k in range(COUNT):
        for j in range(CHUNKS + 1):
            twin_copy(k, j).wait_send()


def local(projections, row_weights, partner):
    rows, width = projections.shape
    block = 2 * rows
    core = lax.axis_index("grp") % 2
    mine = jnp.stack([row_weights.astype(jnp.float32), partner.astype(jnp.float32)])
    mine = jnp.pad(mine, ((0, 6), (0, 0)))
    none = jnp.zeros_like(mine)
    extras = jnp.where(
        core == 0, jnp.concatenate([mine, none], 1), jnp.concatenate([none, mine], 1)
    )
    f32, bf16 = jnp.float32, jnp.bfloat16
    vm, dma = pltpu.VMEM, pltpu.SemaphoreType.DMA
    losses, gradient = pl.pallas_call(
        kernel,
        out_shape=(
            jax.ShapeDtypeStruct((1, rows), f32),
            jax.ShapeDtypeStruct((rows, width), f32),
        ),
        in_specs=[pl.BlockSpec(memory_space=vm)] * 2,
        out_specs=[pl.BlockSpec(memory_space=vm)] * 2,
        scratch_shapes=[
            vm((COUNT, block, width), bf16),
            vm((COUNT, 2, 8, block), f32),
            vm((COUNT, 8, block), f32),
            vm((NSTEP, block, 2 * block), f32),
            vm((2 * NSTEP + 1, block, block), bf16),
            vm((block, 2 * block), f32),
            vm((block, width), f32),
            vm((COUNT, rows, width), f32),
            vm((COUNT, rows, width), bf16),
            vm((COUNT, rows, width), bf16),
            vm((COUNT - 1, rows, width), bf16),
            vm((COUNT, block, 128), f32),
            vm((COUNT, block, 128), f32),
            vm((COUNT, 8, block), f32),
            vm((COUNT, 8, block), f32),
            vm((COUNT, 8, block), f32),
            vm((2, 8, block), f32),
            vm((COUNT - 1, 8, block), f32),
            vm((8, block), f32),
            vm((COUNT, 8, block), f32),
            vm((block, 128), f32),
            vm((COUNT, block, 128), f32),
            dma((COUNT - 1, CHUNKS + 1)), dma((COUNT - 1, CHUNKS + 1)),
            dma((COUNT, CHUNKS + 1)), dma((COUNT, CHUNKS + 1)),
            dma((COUNT - 1, CHUNKS)), dma((COUNT - 1, CHUNKS)),
            dma((COUNT,)), dma((COUNT,)),
            dma, dma,
            dma((COUNT - 1,)), dma((COUNT - 1,)),
            dma((COUNT - 1,)), dma((COUNT - 1,)),
        ],
        compiler_params=pltpu.CompilerParams(
            collective_id=0, has_side_effects=True, vmem_limit_bytes=63 * 2**20
        ),
        cost_estimate=pl.CostEstimate(
            flops=16 * 10**9, bytes_accessed=2 * 10**6, transcendentals=3 * 10**6
        ),
    )(projections, extras)
    return losses.reshape(rows), gradient


def solution(mesh):
    return jax.shard_map(
        local,
        mesh=mesh,
        in_specs=(P(("grp", "dev"), None), P(("grp", "dev")), P(("grp", "dev"))),
        out_specs=(P(("grp", "dev")), P(("grp", "dev"), None)),
        check_vma=False,
    )
```

```python
import jax
import jax.numpy as jnp
from jax import lax
from jax.experimental import pallas as pl
from jax.experimental.pallas import tpu as pltpu
from jax.sharding import PartitionSpec as P

MESH = pl.DeviceIdType.MESH
inv_temp = 10.0
epsilon = 1e-06

SLOTS = (
    (2, 0, 1), (0, 2, 3), (1, 3, 3), (1, 2, 0), (3, 0, 1), (0, 0, 1),
    (0, 0, 3), (0, 3, 3), (1, 1, 0), (3, 0, 0), (0, 0, 0),
)
PARENT = (4, 7, 7, 8, 9, 10, 10, 10, 10, 10)
KIDS = ((0, 0), (0, 0), (0, 0), (0, 0), (0, 1), (0, 0), (0, 0), (1, 3), (3, 4), (4, 5), (5, 10))
SELF = 10
COUNT = 11
STEPS = (
    ((10, 10, 2, 7, 2), (8, 9, 2, 5, 2), (9, 7, 2, 5, 2), (2, 5, 2, 4, 2), (3, 10, 2, 8, 2),
     (6, 8, 2, 5, 1), (8, 2, 2, 1, 2), (1, 9, 2, 4, 2), (0, 2, 2, 1, 1)),
    ((10, 8, 2, 5, 2), (4, 10, 2, 8, 2), (2, 7, 2, 3, 2), (9, 2, 2, 3, 1), (6, 2, 2, 4, 2),
     (5, 7, 2, 1, 1), (3, 4, 2, 0, 2), (0, 10, 2, 5, 1), (6, 1, 1, 0, 1)),
)
NSTEP = 9
ROUNDS = (
    ((9, 0), (7, 0), (8, 0), (5, 0), (9, 1), (7, 1), (8, 1), (5, 1), (9, 2), (7, 2), (8, 2), (5, 2)),
    (),
    ((4, 0), (2, 0), (3, 0), (6, 0), (1, 0)),
    ((4, 1), (2, 1), (3, 1), (6, 1), (1, 1)),
    ((4, 2), (0, 0), (2, 2), (3, 2), (6, 2), (1, 2)),
    (),
    ((0, 1),),
    (),
    ((0, 2),),
    (), (), (), (),
)
ROUND_STEP = (
    (0, 1, 2, -1, 3, 4, 5, 6, 7, 8, -1, -1, -1),
    (0, -1, -1, -1, 1, 2, 3, 4, 5, 6, 7, 8, -1),
)
ZERO = 2 * NSTEP
CHUNKS = 3
PB = 96
RB = 96

NT = (((1,), (1,)), ((), ()))
NN = (((1,), (0,)), ((), ()))
TN = (((0,), (0,)), ((), ()))


def diff(a, b):
    return tuple((x - y) % 4 for x, y in zip(a, b))


def neg(a):
    return tuple(-x % 4 for x in a)


EDGE = tuple(diff(SLOTS[k], SLOTS[PARENT[k]]) for k in range(COUNT - 1))
GREET = tuple(sorted(set(EDGE)))


ORDER = (4, 9, 6, 0, 2, 3, 1, 7, 5, 8, 10)


def backward_plan():
    out = []
    for steps in STEPS:
        prep, rows, cols, cols_a = [], [], [], []
        pb, rb, cb = [0], [0], [0]
        for k in ORDER:
            mine = []
            for t, (a, b1, _, b2, _) in enumerate(steps):
                if k in (a, b1, b2) and t not in prep:
                    prep.append(t)
                if a == k:
                    rows.append(t)
                for u, b in ((0, b1), (1, b2)):
                    if b == k and a != b:
                        mine.append((2 * t + u, a))
            if len(mine) % 2:
                mine.append((ZERO, SELF))
            for i in range(0, len(mine), 2):
                cols.append((mine[i][0], mine[i + 1][0], mine[i][1], mine[i + 1][1]))
            pb.append(len(prep))
            rb.append(len(rows))
            cb.append(len(cols))
        out.append((prep, rows, cols, pb, rb, cb))
    return out


PLAN = backward_plan()

UP_AFTER = (
    (),
    (),
    (),
    ((6, 0), (6, 1), (6, 2)),
    ((0, 0), (0, 1), (0, 2)),
    ((2, 0), (2, 1), (2, 2)),
    ((3, 0), (4, 0), (3, 1), (3, 2)),
    ((1, 0), (1, 1), (4, 1), (1, 2)),
    ((4, 2), (9, 0)),
    ((7, 0), (9, 1), (5, 0), (5, 1), (5, 2), (7, 1), (8, 0), (8, 1), (8, 2), (9, 2)),
    ((7, 2),),
)
UPS = tuple(e for l in UP_AFTER for e in l)
UP_BOUND = tuple(sum(len(l) for l in UP_AFTER[:i]) for i in range(COUNT + 1))


def words(table):
    out = []
    for n in range(0, len(table), 8):
        w = sum(v << (4 * m) for m, v in enumerate(table[n : n + 8]))
        out.append(w - 2**32 if w >= 2**31 else w)
    return out


def lut(i, table):
    if max(table) > 15:
        return lut(i, [v % 16 for v in table]) + 16 * lut(i, [v // 16 for v in table])
    return pick(i, [jnp.int32(w) for w in words(table)])


def lut2(i, c, t0, t1):
    n = max(len(t0), len(t1))
    t0 = tuple(t0) + (0,) * (n - len(t0))
    t1 = tuple(t1) + (0,) * (n - len(t1))
    if max(t0 + t1) > 15:
        low, high = ([[v % 16 for v in t] for t in (t0, t1)], [[v // 16 for v in t] for t in (t0, t1)])
        return lut2(i, c, *low) + 16 * lut2(i, c, *high)
    return pick(i, [jnp.where(c == 0, jnp.int32(a), jnp.int32(b)) for a, b in zip(words(t0), words(t1))])


def pick(i, ws):
    i = jnp.asarray(i, jnp.int32)
    v = ws[0]
    for n in range(1, len(ws)):
        v = jnp.where(i >= 8 * n, ws[n], v)
    return (v >> ((i % 8) * 4)) % 16


def kernel(
    x_ref, w_ref, partner_ref, loss_ref, grad_ref,
    V, XT, XB, E, C, S, acc, H, TX, RX, RC, rsum, rpos, csum, cpos, SO, SI, SR, AO, AR, acol, wcol,
    gs, gr, ss, sr, us, ur, ts, tr, ms, mr, ps, pr, qs, qr,
):
    rows, width = x_ref.shape
    block = 2 * rows
    part = rows // CHUNKS
    grp = lax.axis_index("grp")
    dev = lax.axis_index("dev")
    c = grp % 2
    px, py, pz = (grp // 2) * 2 + dev // 16, (dev // 4) % 4, dev % 4

    def device(d, core):
        x, y, z = (px + d[0]) % 4, (py + d[1]) % 4, (pz + d[2]) % 4
        return ((x // 2) * 2 + core, (x % 2) * 16 + y * 4 + z)

    sibling = device((0, 0, 0), 1 - c)

    barrier = pltpu.get_barrier_semaphore()
    for d in GREET:
        pl.semaphore_signal(barrier, inc=1, device_id=device(d, c), device_id_type=MESH)
    pl.semaphore_signal(barrier, inc=1, device_id=sibling, device_id_type=MESH)

    def base_of(k):
        x = (px + lut(k, [d[0] for d in SLOTS])) % 4
        y = (py + lut(k, [d[1] for d in SLOTS])) % 4
        z = (pz + lut(k, [d[2] for d in SLOTS])) % 4
        return ((x // 2) * 64 + (x % 2) * 16 + y * 4 + z) * rows

    own = pl.multiple_of(c * rows, 64)
    other = pl.multiple_of((1 - c) * rows, 64)

    def norm_body(i, _):
        r = pl.multiple_of(i * 32, 32)
        x = x_ref[pl.ds(r, 32), :]
        inv = lax.rsqrt(jnp.sum(x * x, axis=1, keepdims=True) + epsilon)
        V[SELF, pl.ds(pl.multiple_of(own + r, 32), 32), :] = (x * inv).astype(jnp.bfloat16)
        return 0

    lax.fori_loop(0, rows // 32, norm_body, 0)
    AO[...] = jnp.zeros_like(AO)
    AO[0:1, 0:rows] = w_ref[...].astype(jnp.float32)
    AO[1:2, 0:rows] = partner_ref[...].astype(jnp.float32)
    extras = AO[...]
    XT[SELF, c] = jnp.where(c == 0, extras, pltpu.roll(extras, rows, 1))
    for ref in (rsum, rpos, csum, cpos):
        ref[...] = jnp.zeros_like(ref)

    pl.semaphore_wait(barrier, len(GREET) + 1)

    def piece(k, j, core):
        if j == CHUNKS:
            return XT.at[k, core]
        r = pl.multiple_of(core * rows + j * part, 64)
        return V.at[k, pl.ds(r, part), :]

    def tree_copy(k, j):
        src, dst = piece(PARENT[k], j, c), piece(k, j, c)
        return pltpu.make_async_remote_copy(
            src_ref=src, dst_ref=dst, send_sem=gs.at[k, j], recv_sem=gr.at[k, j],
            device_id=device(neg(EDGE[k]), c), device_id_type=MESH,
        )

    def twin_copy(k, j):
        ref = piece(k, j, c)
        return pltpu.make_async_remote_copy(
            src_ref=ref, dst_ref=ref, send_sem=ss.at[k, j], recv_sem=sr.at[k, j],
            device_id=sibling, device_id_type=MESH,
        )

    def arrive(k, j):
        tree_copy(k, j).wait_recv()
        for child in range(*KIDS[k]):
            tree_copy(child, j).start()
        twin_copy(k, j).start()

    def twins(k):
        for j in range(CHUNKS + 1):
            twin_copy(k, j).wait_recv()
        XB[k] = XT[k, 0] + XT[k, 1]

    for k in (9, 8, 7, 5, 6):
        tree_copy(k, CHUNKS).start()
    for j in range(CHUNKS):
        for k in (9, 8, 7, 5):
            tree_copy(k, j).start()
    for j in range(CHUNKS):
        tree_copy(6, j).start()
    for j in range(CHUNKS + 1):
        twin_copy(SELF, j).start()

    def gate(events):
        for k, j in events:
            if j == 0:
                arrive(k, CHUNKS)
            arrive(k, j)
        for k, j in events:
            if j == CHUNKS - 1:
                twins(k)

    def step_of(t):
        cols = [[[s[n] for s in STEPS[core]] for n in range(5)] for core in (0, 1)]
        a, b1, h1, b2, h2 = (lut2(t, c, cols[0][n], cols[1][n]) for n in range(5))
        return a, b1, h1.astype(jnp.float32) * 0.5, b2, h2.astype(jnp.float32) * 0.5

    lane = lax.broadcasted_iota(jnp.int32, (1, block), 1)
    sub_row = lax.broadcasted_iota(jnp.int32, (RB, 1), 0)
    far = 32 * rows - rows

    def tile_rows(t):
        a, b1, h1, b2, h2 = step_of(t)
        partner = jnp.concatenate([XB[b1, 1:2, :], XB[b2, 1:2, :]], axis=1)
        weight = jnp.concatenate(
            [jnp.full((1, block), h1, jnp.float32), jnp.full((1, block), h2, jnp.float32)], axis=1
        )
        return a, b1, b2, partner, weight

    def row_ids(base, r):
        start = base + r + jnp.where(r >= rows, far, 0)
        return (start + sub_row).astype(jnp.float32)

    def column_ids(b):
        return (base_of(b) + lane + jnp.where(lane >= rows, far, 0)).astype(jnp.float32)

    def score_round(n, _):
        for m, events in enumerate(ROUNDS):
            if events:
                @pl.when(n == m)
                def _(events=events):
                    gate(events)
                    if events == ROUNDS[0]:
                        twins(SELF)
        t = lut2(n, c, [v + 1 for v in ROUND_STEP[0]], [v + 1 for v in ROUND_STEP[1]]) - 1
        pl.when(t >= 0)(lambda: score_step(t))
        return 0

    def score_step(t):
        a, b1, b2, partner, weight = tile_rows(t)
        S[...] = lax.dot_general(
            V[a], jnp.concatenate([V[b1], V[b2]], axis=0), NT, preferred_element_type=jnp.float32
        )
        base = base_of(a)
        ids = jnp.concatenate([column_ids(b1), column_ids(b2)], axis=1)

        offset = inv_temp - jnp.log(weight)
        half1, half2 = weight[0:1, 0:128], weight[0:1, block : block + 128]

        def rows_body(i, carry):
            es, ps_ = carry
            r = pl.multiple_of(i * RB, RB)
            s = S[pl.ds(r, RB), :]
            rid = row_ids(base, r)
            e = jnp.where(rid == ids, 0.0, jnp.exp(s * inv_temp - offset))
            m = jnp.where(rid == partner, s, 0.0)
            E[t, pl.ds(r, RB), :] = e
            er = [e[:, n * 128 : (n + 1) * 128] for n in range(6)]
            mr_ = [m[:, n * 128 : (n + 1) * 128] for n in range(6)]
            rsum[a, pl.ds(r, RB), :] += er[0] + er[1] + er[2] + er[3] + er[4] + er[5]
            rpos[a, pl.ds(r, RB), :] += (mr_[0] + mr_[1] + mr_[2]) * half1 + (mr_[3] + mr_[4] + mr_[5]) * half2
            for n in range(RB // 8):
                es = es + e[n * 8 : (n + 1) * 8, :]
                ps_ = ps_ + m[n * 8 : (n + 1) * 8, :]
            return es, ps_

        zero = jnp.zeros((8, 2 * block), jnp.float32)
        es, ps_ = lax.fori_loop(0, block // RB, rows_body, (zero, zero))
        ps_ = ps_ * weight
        for n, b in ((0, b1), (1, b2)):
            use = jnp.where(a == b, 0.0, 1.0)
            csum[b] += es[:, n * block : (n + 1) * block] * use
            cpos[b] += ps_[:, n * block : (n + 1) * block] * use

    lax.fori_loop(0, 12, score_round, 0)

    def total(rs, cs):
        return jnp.sum(rs.T, axis=0, keepdims=True) + jnp.sum(cs, axis=0, keepdims=True)

    def sums_of(k):
        SO[k] = jnp.concatenate(
            [total(rsum[k], csum[k]), total(rpos[k], cpos[k]), jnp.zeros((6, block), jnp.float32)], axis=0
        )

    def sum_copy(k):
        return pltpu.make_async_remote_copy(
            src_ref=SO.at[k], dst_ref=SR.at[k], send_sem=ps.at[k], recv_sem=pr.at[k],
            device_id=device(SLOTS[k], c), device_id_type=MESH,
        )

    def scale_copy(k):
        return pltpu.make_async_remote_copy(
            src_ref=AO, dst_ref=AR.at[k], send_sem=qs.at[k], recv_sem=qr.at[k],
            device_id=device(neg(SLOTS[k]), c), device_id_type=MESH,
        )

    for k in range(COUNT - 1):
        sums_of(k)
        sum_copy(k).start()
    sums_of(SELF)

    def wide(row):
        return jnp.broadcast_to(row, (128, block)).T

    def wcol_body(k, _):
        wcol[k] = wide(XB[k, 0:1, :])
        return 0

    lax.fori_loop(0, COUNT, wcol_body, 0)
    C[ZERO] = jnp.zeros((block, block), jnp.bfloat16)
    acc[...] = jnp.zeros_like(acc)
    mine = SO[SELF]
    for k in range(COUNT - 1):
        sum_copy(k).wait_recv()
        mine = mine + SR[k]
    SI[0] = mine
    twin_sums = pltpu.make_async_remote_copy(
        src_ref=SI.at[0], dst_ref=SI.at[1], send_sem=ms, recv_sem=mr, device_id=sibling, device_id_type=MESH
    )
    twin_sums.start()
    twin_sums.wait()
    both = SI[0] + SI[1]
    exp_sum, positive = both[0:1, :], both[1:2, :] * inv_temp
    scale = XB[SELF, 0:1, :] / exp_sum
    AO[...] = jnp.broadcast_to(scale, (8, block))
    for k in range(COUNT - 1):
        scale_copy(k).start()
    AR[SELF] = AO[...]
    losses = jnp.broadcast_to(inv_temp + jnp.log(exp_sum) - positive, (8, block))
    loss_ref[...] = jnp.where(c == 0, losses, pltpu.roll(losses, rows, 1))[0:1, :rows]
    for k in range(COUNT - 1):
        scale_copy(k).wait_recv()

    def twin_part(k):
        return pltpu.make_async_remote_copy(
            src_ref=TX.at[k], dst_ref=RX.at[k], send_sem=ts.at[k], recv_sem=tr.at[k],
            device_id=sibling, device_id_type=MESH,
        )

    def up_copy(k, j, d):
        r = pl.multiple_of(j * part, 64)
        return pltpu.make_async_remote_copy(
            src_ref=TX.at[k, pl.ds(r, part), :], dst_ref=RC.at[k, pl.ds(r, part), :],
            send_sem=us.at[k, j], recv_sem=ur.at[k, j], device_id=device(d, c), device_id_type=MESH,
        )

    def edge_of(k):
        return tuple(lut(k, [e[n] for e in EDGE]) for n in range(3))

    def gathered(k, j, lo, hi):
        r = pl.multiple_of(j * part, 64)

        def child(n, _):
            up_copy(n, j, (0, 0, 1)).wait_recv()
            H[k, pl.ds(r, part), :] += RC[n, pl.ds(r, part), :].astype(jnp.float32)
            return 0

        lax.fori_loop(lo, hi, child, 0)

    def up_event(ev, _):
        k = lut(ev, [e[0] for e in UPS])
        j = lut(ev, [e[1] for e in UPS])

        @pl.when(j == 0)
        def _():
            twin_part(k).wait()

        gathered(k, j, lut(k, [a for a, _ in KIDS]), lut(k, [b for _, b in KIDS]))
        r = pl.multiple_of(j * part, 64)
        TX[k, pl.ds(r, part), :] = (
            H[k, pl.ds(r, part), :] + RX[k, pl.ds(r, part), :].astype(jnp.float32)
        ).astype(jnp.bfloat16)
        up_copy(k, j, edge_of(k)).start()
        return 0

    def prepare(n, _):
        t = lut2(n, c, PLAN[0][0], PLAN[1][0])
        a, b1, b2, partner, weight = tile_rows(t)
        base = base_of(a)
        acol[...] = wide(AR[a, 0:1, :])
        arow = jnp.concatenate([AR[b1, 0:1, :], AR[b2, 0:1, :]], axis=1)
        wrow = jnp.concatenate([XB[b1, 0:1, :], XB[b2, 0:1, :]], axis=1)

        def rows_body(i, _):
            r = pl.multiple_of(i * PB, PB)
            rid = row_ids(base, r)[:PB]
            ac, wc = acol[pl.ds(r, PB), :], wcol[a, pl.ds(r, PB), :]
            ac = jnp.concatenate([ac] * (2 * block // 128), axis=1)
            wc = jnp.concatenate([wc] * (2 * block // 128), axis=1)
            v = E[t, pl.ds(r, PB), :] * (ac + arow)
            v = (v - jnp.where(rid == partner, (wc + wrow) * weight, 0.0)).astype(jnp.bfloat16)
            C[2 * t, pl.ds(r, PB), :] = v[:, :block]
            C[2 * t + 1, pl.ds(r, PB), :] = v[:, block:]
            return 0

        lax.fori_loop(0, block // PB, rows_body, 0)
        return 0

    def row_product(n, _):
        t = lut2(n, c, PLAN[0][1], PLAN[1][1])
        _, b1, _, b2, _ = step_of(t)
        acc[...] += lax.dot_general(
            jnp.concatenate([C[2 * t], C[2 * t + 1]], axis=1),
            jnp.concatenate([V[b1], V[b2]], axis=0),
            NN, preferred_element_type=jnp.float32,
        )
        return 0

    def column_product(n, _):
        u1, u2, a1, a2 = (
            lut2(n, c, [q[i] for q in PLAN[0][2]], [q[i] for q in PLAN[1][2]]) for i in range(4)
        )
        acc[...] += lax.dot_general(
            jnp.concatenate([C[u1], C[u2]], axis=0),
            jnp.concatenate([V[a1], V[a2]], axis=0),
            TN, preferred_element_type=jnp.float32,
        )
        return 0

    def slot_body(i, _):
        k = lut(i, ORDER)
        for n, body in ((3, prepare), (4, row_product), (5, column_product)):
            lo = lut2(i, c, PLAN[0][n][:-1], PLAN[1][n][:-1])
            hi = lut2(i, c, PLAN[0][n][1:], PLAN[1][n][1:])
            lax.fori_loop(lo, hi, body, 0)

        def split(n, _):
            r = pl.multiple_of(n * 32, 32)
            theirs = pl.ds(pl.multiple_of(other + r, 32), 32)
            ours = pl.ds(pl.multiple_of(own + r, 32), 32)
            TX[k, pl.ds(r, 32), :] = acc[theirs, :].astype(jnp.bfloat16)
            H[k, pl.ds(r, 32), :] = acc[ours, :]
            zero = jnp.zeros((32, width), jnp.float32)
            acc[theirs, :] = zero
            acc[ours, :] = zero
            return 0

        lax.fori_loop(0, rows // 32, split, 0)
        twin_part(k).start()
        first = lut(i, UP_BOUND[:-1])
        count = lut(i, [len(u) for u in UP_AFTER])
        lax.fori_loop(first, first + count, up_event, 0)
        return 0

    lax.fori_loop(0, COUNT, slot_body, 0)

    twin_part(SELF).wait()

    def finish(j, _):
        gathered(SELF, j, *KIDS[SELF])

        def body(i, _):
            r = pl.multiple_of(j * part + i * 16, 16)
            x = x_ref[pl.ds(r, 16), :]
            inv = lax.rsqrt(jnp.sum(x * x, axis=1, keepdims=True) + epsilon)
            unit = x * inv
            dview = (H[SELF, pl.ds(r, 16), :] + RX[SELF, pl.ds(r, 16), :].astype(jnp.float32)) * inv_temp
            grad_ref[pl.ds(r, 16), :] = inv * (
                dview - unit * jnp.sum(unit * dview, axis=1, keepdims=True)
            )
            return 0

        lax.fori_loop(0, part // 16, body, 0)
        return 0

    lax.fori_loop(0, CHUNKS, finish, 0)

    for k in range(COUNT - 1):
        for j in range(CHUNKS + 1):
            tree_copy(k, j).wait_send()
        for j in range(CHUNKS):
            up_copy(k, j, EDGE[k]).wait_send()
        sum_copy(k).wait_send()
        scale_copy(k).wait_send()
    for k in range(COUNT):
        for j in range(CHUNKS + 1):
            twin_copy(k, j).wait_send()


def local(projections, row_weights, partner):
    rows, width = projections.shape
    block = 2 * rows
    f32, bf16 = jnp.float32, jnp.bfloat16
    vm, dma = pltpu.VMEM, pltpu.SemaphoreType.DMA
    losses, gradient = pl.pallas_call(
        kernel,
        out_shape=(
            jax.ShapeDtypeStruct((1, rows), f32),
            jax.ShapeDtypeStruct((rows, width), f32),
        ),
        in_specs=[pl.BlockSpec(memory_space=vm)] * 3,
        out_specs=[pl.BlockSpec(memory_space=vm)] * 2,
        scratch_shapes=[
            vm((COUNT, block, width), bf16),
            vm((COUNT, 2, 8, block), f32),
            vm((COUNT, 8, block), f32),
            vm((NSTEP, block, 2 * block), f32),
            vm((2 * NSTEP + 1, block, block), bf16),
            vm((block, 2 * block), f32),
            vm((block, width), f32),
            vm((COUNT, rows, width), f32),
            vm((COUNT, rows, width), bf16),
            vm((COUNT, rows, width), bf16),
            vm((COUNT - 1, rows, width), bf16),
            vm((COUNT, block, 128), f32),
            vm((COUNT, block, 128), f32),
            vm((COUNT, 8, block), f32),
            vm((COUNT, 8, block), f32),
            vm((COUNT, 8, block), f32),
            vm((2, 8, block), f32),
            vm((COUNT - 1, 8, block), f32),
            vm((8, block), f32),
            vm((COUNT, 8, block), f32),
            vm((block, 128), f32),
            vm((COUNT, block, 128), f32),
            dma((COUNT - 1, CHUNKS + 1)), dma((COUNT - 1, CHUNKS + 1)),
            dma((COUNT, CHUNKS + 1)), dma((COUNT, CHUNKS + 1)),
            dma((COUNT - 1, CHUNKS)), dma((COUNT - 1, CHUNKS)),
            dma((COUNT,)), dma((COUNT,)),
            dma, dma,
            dma((COUNT - 1,)), dma((COUNT - 1,)),
            dma((COUNT - 1,)), dma((COUNT - 1,)),
        ],
        compiler_params=pltpu.CompilerParams(
            collective_id=0, has_side_effects=True, vmem_limit_bytes=63 * 2**20
        ),
        cost_estimate=pl.CostEstimate(
            flops=16 * 10**9, bytes_accessed=2 * 10**6, transcendentals=3 * 10**6
        ),
    )(projections, row_weights.reshape(1, rows), partner.reshape(1, rows))
    return losses.reshape(rows), gradient


def solution(mesh):
    return jax.shard_map(
        local,
        mesh=mesh,
        in_specs=(P(("grp", "dev"), None), P(("grp", "dev")), P(("grp", "dev"))),
        out_specs=(P(("grp", "dev")), P(("grp", "dev"), None)),
        check_vma=False,
    )
```

```python
import jax
import jax.numpy as jnp
from jax import lax
from jax.experimental import pallas as pl
from jax.experimental.pallas import tpu as pltpu
from jax.sharding import PartitionSpec as P

MESH = pl.DeviceIdType.MESH
inv_temp = 10.0
epsilon = 1e-06

SLOTS = (
    (2, 0, 1), (0, 2, 3), (1, 3, 3), (1, 2, 0), (3, 0, 1), (0, 0, 1),
    (0, 0, 3), (0, 3, 3), (1, 1, 0), (3, 0, 0), (0, 0, 0),
)
PARENT = (4, 7, 7, 8, 9, 10, 10, 10, 10, 10)
KIDS = ((0, 0), (0, 0), (0, 0), (0, 0), (0, 1), (0, 0), (0, 0), (1, 3), (3, 4), (4, 5), (5, 10))
SELF = 10
COUNT = 11
STEPS = (
    ((10, 10, 2, 7, 2), (8, 9, 2, 5, 2), (9, 7, 2, 5, 2), (2, 5, 2, 4, 2), (3, 10, 2, 8, 2),
     (6, 8, 2, 5, 1), (8, 2, 2, 1, 2), (1, 9, 2, 4, 2), (0, 2, 2, 1, 1)),
    ((10, 8, 2, 5, 2), (4, 10, 2, 8, 2), (2, 7, 2, 3, 2), (9, 2, 2, 3, 1), (6, 2, 2, 4, 2),
     (5, 7, 2, 1, 1), (3, 4, 2, 0, 2), (0, 10, 2, 5, 1), (6, 1, 1, 0, 1)),
)
NSTEP = 9
ROUNDS = (
    ((9, 0), (7, 0), (8, 0), (5, 0), (9, 1), (7, 1), (8, 1), (5, 1), (9, 2), (7, 2), (8, 2), (5, 2)),
    (),
    ((4, 0), (2, 0), (3, 0), (6, 0), (1, 0)),
    ((4, 1), (2, 1), (3, 1), (6, 1), (1, 1)),
    ((4, 2), (0, 0), (2, 2), (3, 2), (6, 2), (1, 2)),
    (),
    ((0, 1),),
    (),
    ((0, 2),),
    (), (), (), (),
)
ROUND_STEP = (
    (0, 1, 2, -1, 3, 4, 5, 6, 7, 8, -1, -1, -1),
    (0, -1, -1, -1, 1, 2, 3, 4, 5, 6, 7, 8, -1),
)
ZERO = 2 * NSTEP
CHUNKS = 3
PB = 96
RB = 96

NT = (((1,), (1,)), ((), ()))
NN = (((1,), (0,)), ((), ()))
TN = (((0,), (0,)), ((), ()))


def diff(a, b):
    return tuple((x - y) % 4 for x, y in zip(a, b))


def neg(a):
    return tuple(-x % 4 for x in a)


EDGE = tuple(diff(SLOTS[k], SLOTS[PARENT[k]]) for k in range(COUNT - 1))
GREET = tuple(sorted(set(EDGE)))


ORDER = (4, 9, 6, 0, 2, 3, 1, 7, 5, 8, 10)


def backward_plan():
    out = []
    for steps in STEPS:
        prep, rows, cols, cols_a = [], [], [], []
        pb, rb, cb = [0], [0], [0]
        for k in ORDER:
            mine = []
            for t, (a, b1, _, b2, _) in enumerate(steps):
                if k in (a, b1, b2) and t not in prep:
                    prep.append(t)
                if a == k:
                    rows.append(t)
                for u, b in ((0, b1), (1, b2)):
                    if b == k and a != b:
                        mine.append((2 * t + u, a))
            if len(mine) % 2:
                mine.append((ZERO, SELF))
            for i in range(0, len(mine), 2):
                cols.append((mine[i][0], mine[i + 1][0], mine[i][1], mine[i + 1][1]))
            pb.append(len(prep))
            rb.append(len(rows))
            cb.append(len(cols))
        out.append((prep, rows, cols, pb, rb, cb))
    return out


PLAN = backward_plan()

UP_AFTER = (
    (),
    (),
    (),
    ((6, 0), (6, 1), (6, 2)),
    ((0, 0), (0, 1), (0, 2)),
    ((2, 0), (2, 1), (2, 2)),
    ((3, 0), (4, 0), (3, 1), (3, 2)),
    ((1, 0), (1, 1), (4, 1), (1, 2)),
    ((4, 2), (9, 0)),
    ((7, 0), (9, 1), (5, 0), (5, 1), (5, 2), (7, 1), (8, 0), (8, 1), (8, 2), (9, 2)),
    ((7, 2),),
)
UPS = tuple(e for l in UP_AFTER for e in l)
UP_BOUND = tuple(sum(len(l) for l in UP_AFTER[:i]) for i in range(COUNT + 1))


def words(table):
    out = []
    for n in range(0, len(table), 8):
        w = sum(v << (4 * m) for m, v in enumerate(table[n : n + 8]))
        out.append(w - 2**32 if w >= 2**31 else w)
    return out


def lut(i, table):
    if max(table) > 15:
        return lut(i, [v % 16 for v in table]) + 16 * lut(i, [v // 16 for v in table])
    return pick(i, [jnp.int32(w) for w in words(table)])


def lut2(i, c, t0, t1):
    n = max(len(t0), len(t1))
    t0 = tuple(t0) + (0,) * (n - len(t0))
    t1 = tuple(t1) + (0,) * (n - len(t1))
    if max(t0 + t1) > 15:
        low, high = ([[v % 16 for v in t] for t in (t0, t1)], [[v // 16 for v in t] for t in (t0, t1)])
        return lut2(i, c, *low) + 16 * lut2(i, c, *high)
    return pick(i, [jnp.where(c == 0, jnp.int32(a), jnp.int32(b)) for a, b in zip(words(t0), words(t1))])


def pick(i, ws):
    i = jnp.asarray(i, jnp.int32)
    v = ws[0]
    for n in range(1, len(ws)):
        v = jnp.where(i >= 8 * n, ws[n], v)
    return (v >> ((i % 8) * 4)) % 16


def kernel(
    x_ref, w_ref, partner_ref, loss_ref, grad_ref,
    V, XT, XB, E, C, S, acc, H, TX, RX, RC, rsum, rpos, csum, cpos, SO, SI, SR, AO, AR, acol, wcol,
    gs, gr, ss, sr, us, ur, ts, tr, ms, mr, ps, pr, qs, qr,
):
    rows, width = x_ref.shape
    block = 2 * rows
    part = rows // CHUNKS
    grp = lax.axis_index("grp")
    dev = lax.axis_index("dev")
    c = grp % 2
    px, py, pz = (grp // 2) * 2 + dev // 16, (dev // 4) % 4, dev % 4

    def device(d, core):
        x, y, z = (px + d[0]) % 4, (py + d[1]) % 4, (pz + d[2]) % 4
        return ((x // 2) * 2 + core, (x % 2) * 16 + y * 4 + z)

    sibling = device((0, 0, 0), 1 - c)

    barrier = pltpu.get_barrier_semaphore()
    for d in GREET:
        pl.semaphore_signal(barrier, inc=1, device_id=device(d, c), device_id_type=MESH)
    pl.semaphore_signal(barrier, inc=1, device_id=sibling, device_id_type=MESH)

    def base_of(k):
        x = (px + lut(k, [d[0] for d in SLOTS])) % 4
        y = (py + lut(k, [d[1] for d in SLOTS])) % 4
        z = (pz + lut(k, [d[2] for d in SLOTS])) % 4
        return ((x // 2) * 64 + (x % 2) * 16 + y * 4 + z) * rows

    own = pl.multiple_of(c * rows, 64)
    other = pl.multiple_of((1 - c) * rows, 64)

    def norm_body(i, _):
        r = pl.multiple_of(i * 32, 32)
        x = x_ref[pl.ds(r, 32), :]
        inv = lax.rsqrt(jnp.sum(x * x, axis=1, keepdims=True) + epsilon)
        V[SELF, pl.ds(pl.multiple_of(own + r, 32), 32), :] = (x * inv).astype(jnp.bfloat16)
        return 0

    lax.fori_loop(0, rows // 32, norm_body, 0)
    AO[...] = jnp.zeros_like(AO)
    AO[0:1, 0:rows] = w_ref[...].astype(jnp.float32)
    AO[1:2, 0:rows] = partner_ref[...].astype(jnp.float32)
    extras = AO[...]
    XT[SELF, c] = jnp.where(c == 0, extras, pltpu.roll(extras, rows, 1))
    for ref in (rsum, rpos, csum, cpos):
        ref[...] = jnp.zeros_like(ref)

    pl.semaphore_wait(barrier, len(GREET) + 1)

    def piece(k, j, core):
        if j == CHUNKS:
            return XT.at[k, core]
        r = pl.multiple_of(core * rows + j * part, 64)
        return V.at[k, pl.ds(r, part), :]

    def tree_copy(k, j):
        src, dst = piece(PARENT[k], j, c), piece(k, j, c)
        return pltpu.make_async_remote_copy(
            src_ref=src, dst_ref=dst, send_sem=gs.at[k, j], recv_sem=gr.at[k, j],
            device_id=device(neg(EDGE[k]), c), device_id_type=MESH,
        )

    def twin_copy(k, j):
        ref = piece(k, j, c)
        return pltpu.make_async_remote_copy(
            src_ref=ref, dst_ref=ref, send_sem=ss.at[k, j], recv_sem=sr.at[k, j],
            device_id=sibling, device_id_type=MESH,
        )

    def arrive(k, j):
        tree_copy(k, j).wait_recv()
        for child in range(*KIDS[k]):
            tree_copy(child, j).start()
        twin_copy(k, j).start()

    def twins(k):
        for j in range(CHUNKS + 1):
            twin_copy(k, j).wait_recv()
        XB[k] = XT[k, 0] + XT[k, 1]

    for k in (9, 8, 7, 5, 6):
        tree_copy(k, CHUNKS).start()
    for j in range(CHUNKS):
        for k in (9, 8, 7, 5):
            tree_copy(k, j).start()
    for j in range(CHUNKS):
        tree_copy(6, j).start()
    for j in range(CHUNKS + 1):
        twin_copy(SELF, j).start()

    def gate(events):
        for k, j in events:
            if j == 0:
                arrive(k, CHUNKS)
            arrive(k, j)
        for k, j in events:
            if j == CHUNKS - 1:
                twins(k)

    def step_of(t):
        cols = [[[s[n] for s in STEPS[core]] for n in range(5)] for core in (0, 1)]
        a, b1, h1, b2, h2 = (lut2(t, c, cols[0][n], cols[1][n]) for n in range(5))
        return a, b1, h1.astype(jnp.float32) * 0.5, b2, h2.astype(jnp.float32) * 0.5

    lane = lax.broadcasted_iota(jnp.int32, (1, block), 1)
    sub_row = lax.broadcasted_iota(jnp.int32, (RB, 1), 0)
    far = 32 * rows - rows

    def tile_rows(t):
        a, b1, h1, b2, h2 = step_of(t)
        partner = jnp.concatenate([XB[b1, 1:2, :], XB[b2, 1:2, :]], axis=1)
        weight = jnp.concatenate(
            [jnp.full((1, block), h1, jnp.float32), jnp.full((1, block), h2, jnp.float32)], axis=1
        )
        return a, b1, b2, partner, weight

    def row_ids(base, r):
        start = base + r + jnp.where(r >= rows, far, 0)
        return (start + sub_row).astype(jnp.float32)

    def column_ids(b):
        return (base_of(b) + lane + jnp.where(lane >= rows, far, 0)).astype(jnp.float32)

    def score_round(n, _):
        for m, events in enumerate(ROUNDS):
            if events:
                @pl.when(n == m)
                def _(events=events):
                    gate(events)
                    if events == ROUNDS[0]:
                        twins(SELF)
        t = lut2(n, c, [v + 1 for v in ROUND_STEP[0]], [v + 1 for v in ROUND_STEP[1]]) - 1
        pl.when(t >= 0)(lambda: score_step(t))
        return 0

    def score_step(t):
        a, b1, b2, partner, weight = tile_rows(t)
        S[...] = lax.dot_general(
            V[a], jnp.concatenate([V[b1], V[b2]], axis=0), NT, preferred_element_type=jnp.float32
        )
        base = base_of(a)
        ids = jnp.concatenate([column_ids(b1), column_ids(b2)], axis=1)

        offset = inv_temp - jnp.log(weight)
        half1, half2 = weight[0:1, 0:128], weight[0:1, block : block + 128]

        def rows_body(i, carry):
            es, ps_ = carry
            r = pl.multiple_of(i * RB, RB)
            s = S[pl.ds(r, RB), :]
            rid = row_ids(base, r)
            e = jnp.where(rid == ids, 0.0, jnp.exp(s * inv_temp - offset))
            m = jnp.where(rid == partner, s, 0.0)
            E[t, pl.ds(r, RB), :] = e
            er = [e[:, n * 128 : (n + 1) * 128] for n in range(6)]
            mr_ = [m[:, n * 128 : (n + 1) * 128] for n in range(6)]
            rsum[a, pl.ds(r, RB), :] += er[0] + er[1] + er[2] + er[3] + er[4] + er[5]
            rpos[a, pl.ds(r, RB), :] += (mr_[0] + mr_[1] + mr_[2]) * half1 + (mr_[3] + mr_[4] + mr_[5]) * half2
            for n in range(RB // 8):
                es = es + e[n * 8 : (n + 1) * 8, :]
                ps_ = ps_ + m[n * 8 : (n + 1) * 8, :]
            return es, ps_

        zero = jnp.zeros((8, 2 * block), jnp.float32)
        es, ps_ = lax.fori_loop(0, block // RB, rows_body, (zero, zero))
        ps_ = ps_ * weight
        for n, b in ((0, b1), (1, b2)):
            use = jnp.where(a == b, 0.0, 1.0)
            csum[b] += es[:, n * block : (n + 1) * block] * use
            cpos[b] += ps_[:, n * block : (n + 1) * block] * use

    lax.fori_loop(0, 12, score_round, 0)

    def total(rs, cs):
        return jnp.sum(rs.T, axis=0, keepdims=True) + jnp.sum(cs, axis=0, keepdims=True)

    def sums_of(k):
        SO[k] = jnp.concatenate(
            [total(rsum[k], csum[k]), total(rpos[k], cpos[k]), jnp.zeros((6, block), jnp.float32)], axis=0
        )

    def sum_copy(k):
        return pltpu.make_async_remote_copy(
            src_ref=SO.at[k], dst_ref=SR.at[k], send_sem=ps.at[k], recv_sem=pr.at[k],
            device_id=device(SLOTS[k], c), device_id_type=MESH,
        )

    def scale_copy(k):
        return pltpu.make_async_remote_copy(
            src_ref=AO, dst_ref=AR.at[k], send_sem=qs.at[k], recv_sem=qr.at[k],
            device_id=device(neg(SLOTS[k]), c), device_id_type=MESH,
        )

    for k in range(COUNT - 1):
        sums_of(k)
        sum_copy(k).start()
    sums_of(SELF)

    def wide(row):
        return jnp.broadcast_to(row, (128, block)).T

    def wcol_body(k, _):
        wcol[k] = wide(XB[k, 0:1, :])
        return 0

    lax.fori_loop(0, COUNT, wcol_body, 0)
    C[ZERO] = jnp.zeros((block, block), jnp.bfloat16)
    acc[...] = jnp.zeros_like(acc)
    mine = SO[SELF]
    for k in range(COUNT - 1):
        sum_copy(k).wait_recv()
        mine = mine + SR[k]
    SI[0] = mine
    twin_sums = pltpu.make_async_remote_copy(
        src_ref=SI.at[0], dst_ref=SI.at[1], send_sem=ms, recv_sem=mr, device_id=sibling, device_id_type=MESH
    )
    twin_sums.start()
    twin_sums.wait()
    both = SI[0] + SI[1]
    exp_sum, positive = both[0:1, :], both[1:2, :] * inv_temp
    scale = XB[SELF, 0:1, :] / exp_sum
    AO[...] = jnp.broadcast_to(scale, (8, block))
    for k in range(COUNT - 1):
        scale_copy(k).start()
    AR[SELF] = AO[...]
    losses = jnp.broadcast_to(inv_temp + jnp.log(exp_sum) - positive, (8, block))
    loss_ref[...] = jnp.where(c == 0, losses, pltpu.roll(losses, rows, 1))[0:1, :rows]
    for k in range(COUNT):
        for j in range(CHUNKS + 1):
            if k < SELF:
                tree_copy(k, j).wait_send()
            twin_copy(k, j).wait_send()
    for k in range(COUNT - 1):
        sum_copy(k).wait_send()
    for k in range(COUNT - 1):
        scale_copy(k).wait_recv()

    def twin_part(k):
        return pltpu.make_async_remote_copy(
            src_ref=TX.at[k], dst_ref=RX.at[k], send_sem=ts.at[k], recv_sem=tr.at[k],
            device_id=sibling, device_id_type=MESH,
        )

    def up_copy(k, j, d):
        r = pl.multiple_of(j * part, 64)
        return pltpu.make_async_remote_copy(
            src_ref=TX.at[k, pl.ds(r, part), :], dst_ref=RC.at[k, pl.ds(r, part), :],
            send_sem=us.at[k, j], recv_sem=ur.at[k, j], device_id=device(d, c), device_id_type=MESH,
        )

    def edge_of(k):
        return tuple(lut(k, [e[n] for e in EDGE]) for n in range(3))

    def gathered(k, j, lo, hi):
        r = pl.multiple_of(j * part, 64)

        def child(n, _):
            up_copy(n, j, (0, 0, 1)).wait_recv()
            H[k, pl.ds(r, part), :] += RC[n, pl.ds(r, part), :].astype(jnp.float32)
            return 0

        lax.fori_loop(lo, hi, child, 0)

    def up_event(ev, _):
        k = lut(ev, [e[0] for e in UPS])
        j = lut(ev, [e[1] for e in UPS])

        @pl.when(j == 0)
        def _():
            twin_part(k).wait()

        gathered(k, j, lut(k, [a for a, _ in KIDS]), lut(k, [b for _, b in KIDS]))
        r = pl.multiple_of(j * part, 64)
        TX[k, pl.ds(r, part), :] = (
            H[k, pl.ds(r, part), :] + RX[k, pl.ds(r, part), :].astype(jnp.float32)
        ).astype(jnp.bfloat16)
        up_copy(k, j, edge_of(k)).start()
        return 0

    def prepare(n, _):
        t = lut2(n, c, PLAN[0][0], PLAN[1][0])
        a, b1, b2, partner, weight = tile_rows(t)
        base = base_of(a)
        acol[...] = wide(AR[a, 0:1, :])
        arow = jnp.concatenate([AR[b1, 0:1, :], AR[b2, 0:1, :]], axis=1)
        wrow = jnp.concatenate([XB[b1, 0:1, :], XB[b2, 0:1, :]], axis=1)

        def rows_body(i, _):
            r = pl.multiple_of(i * PB, PB)
            rid = row_ids(base, r)[:PB]
            ac, wc = acol[pl.ds(r, PB), :], wcol[a, pl.ds(r, PB), :]
            ac = jnp.concatenate([ac] * (2 * block // 128), axis=1)
            wc = jnp.concatenate([wc] * (2 * block // 128), axis=1)
            v = E[t, pl.ds(r, PB), :] * (ac + arow)
            v = (v - jnp.where(rid == partner, (wc + wrow) * weight, 0.0)).astype(jnp.bfloat16)
            C[2 * t, pl.ds(r, PB), :] = v[:, :block]
            C[2 * t + 1, pl.ds(r, PB), :] = v[:, block:]
            return 0

        lax.fori_loop(0, block // PB, rows_body, 0)
        return 0

    def row_product(n, _):
        t = lut2(n, c, PLAN[0][1], PLAN[1][1])
        _, b1, _, b2, _ = step_of(t)
        acc[...] += lax.dot_general(
            jnp.concatenate([C[2 * t], C[2 * t + 1]], axis=1),
            jnp.concatenate([V[b1], V[b2]], axis=0),
            NN, preferred_element_type=jnp.float32,
        )
        return 0

    def column_product(n, _):
        u1, u2, a1, a2 = (
            lut2(n, c, [q[i] for q in PLAN[0][2]], [q[i] for q in PLAN[1][2]]) for i in range(4)
        )
        acc[...] += lax.dot_general(
            jnp.concatenate([C[u1], C[u2]], axis=0),
            jnp.concatenate([V[a1], V[a2]], axis=0),
            TN, preferred_element_type=jnp.float32,
        )
        return 0

    def slot_body(i, _):
        k = lut(i, ORDER)
        for n, body in ((3, prepare), (4, row_product), (5, column_product)):
            lo = lut2(i, c, PLAN[0][n][:-1], PLAN[1][n][:-1])
            hi = lut2(i, c, PLAN[0][n][1:], PLAN[1][n][1:])
            lax.fori_loop(lo, hi, body, 0)

        def split(n, _):
            r = pl.multiple_of(n * 32, 32)
            theirs = pl.ds(pl.multiple_of(other + r, 32), 32)
            ours = pl.ds(pl.multiple_of(own + r, 32), 32)
            TX[k, pl.ds(r, 32), :] = acc[theirs, :].astype(jnp.bfloat16)
            H[k, pl.ds(r, 32), :] = acc[ours, :]
            zero = jnp.zeros((32, width), jnp.float32)
            acc[theirs, :] = zero
            acc[ours, :] = zero
            return 0

        lax.fori_loop(0, rows // 32, split, 0)
        twin_part(k).start()
        first = lut(i, UP_BOUND[:-1])
        count = lut(i, [len(u) for u in UP_AFTER])
        lax.fori_loop(first, first + count, up_event, 0)
        return 0

    lax.fori_loop(0, COUNT, slot_body, 0)

    twin_part(SELF).wait()

    def finish(j, _):
        gathered(SELF, j, *KIDS[SELF])

        def body(i, _):
            r = pl.multiple_of(j * part + i * 16, 16)
            x = x_ref[pl.ds(r, 16), :]
            inv = lax.rsqrt(jnp.sum(x * x, axis=1, keepdims=True) + epsilon)
            unit = x * inv
            dview = (H[SELF, pl.ds(r, 16), :] + RX[SELF, pl.ds(r, 16), :].astype(jnp.float32)) * inv_temp
            grad_ref[pl.ds(r, 16), :] = inv * (
                dview - unit * jnp.sum(unit * dview, axis=1, keepdims=True)
            )
            return 0

        lax.fori_loop(0, part // 16, body, 0)
        return 0

    lax.fori_loop(0, CHUNKS, finish, 0)

    for k in range(COUNT - 1):
        for j in range(CHUNKS):
            up_copy(k, j, EDGE[k]).wait_send()
        scale_copy(k).wait_send()


def local(projections, row_weights, partner):
    rows, width = projections.shape
    block = 2 * rows
    f32, bf16 = jnp.float32, jnp.bfloat16
    vm, dma = pltpu.VMEM, pltpu.SemaphoreType.DMA
    losses, gradient = pl.pallas_call(
        kernel,
        out_shape=(
            jax.ShapeDtypeStruct((1, rows), f32),
            jax.ShapeDtypeStruct((rows, width), f32),
        ),
        in_specs=[pl.BlockSpec(memory_space=vm)] * 3,
        out_specs=[pl.BlockSpec(memory_space=vm)] * 2,
        scratch_shapes=[
            vm((COUNT, block, width), bf16),
            vm((COUNT, 2, 8, block), f32),
            vm((COUNT, 8, block), f32),
            vm((NSTEP, block, 2 * block), f32),
            vm((2 * NSTEP + 1, block, block), bf16),
            vm((block, 2 * block), f32),
            vm((block, width), f32),
            vm((COUNT, rows, width), f32),
            vm((COUNT, rows, width), bf16),
            vm((COUNT, rows, width), bf16),
            vm((COUNT - 1, rows, width), bf16),
            vm((COUNT, block, 128), f32),
            vm((COUNT, block, 128), f32),
            vm((COUNT, 8, block), f32),
            vm((COUNT, 8, block), f32),
            vm((COUNT, 8, block), f32),
            vm((2, 8, block), f32),
            vm((COUNT - 1, 8, block), f32),
            vm((8, block), f32),
            vm((COUNT, 8, block), f32),
            vm((block, 128), f32),
            vm((COUNT, block, 128), f32),
            dma((COUNT - 1, CHUNKS + 1)), dma((COUNT - 1, CHUNKS + 1)),
            dma((COUNT, CHUNKS + 1)), dma((COUNT, CHUNKS + 1)),
            dma((COUNT - 1, CHUNKS)), dma((COUNT - 1, CHUNKS)),
            dma((COUNT,)), dma((COUNT,)),
            dma, dma,
            dma((COUNT - 1,)), dma((COUNT - 1,)),
            dma((COUNT - 1,)), dma((COUNT - 1,)),
        ],
        compiler_params=pltpu.CompilerParams(
            collective_id=0, has_side_effects=True, vmem_limit_bytes=63 * 2**20
        ),
        cost_estimate=pl.CostEstimate(
            flops=16 * 10**9, bytes_accessed=2 * 10**6, transcendentals=3 * 10**6
        ),
    )(projections, row_weights.reshape(1, rows), partner.reshape(1, rows))
    return losses.reshape(rows), gradient


def solution(mesh):
    return jax.shard_map(
        local,
        mesh=mesh,
        in_specs=(P(("grp", "dev"), None), P(("grp", "dev")), P(("grp", "dev"))),
        out_specs=(P(("grp", "dev")), P(("grp", "dev"), None)),
        check_vma=False,
    )
```
